256 devices in a mesh: row: 8 (over x, z_lo), col: 32 (over z_hi, y, core).
Axes of the slice: x: 4, y: 4, z: 8 (z_hi: 4, z_lo: 2; z = z_hi * 2 + z_lo), core: 2. Of those that a mesh axis runs over, the one named last changes fastest.
Arguments:
- level_set: float32 [12800, 51200], P('row', 'col'), may hold values from -48 to 48
- dose_map: float32 [5120, 20480], P(('row', 'col')), may hold values from 0.6 to 1.6
Outputs:
- exposure: float32 [5120, 20480], P(('row', 'col'))
The draws below stay inside these ranges and needn't reach their ends.
All inputs are finite; a program needn't handle non-finite values.
Results may differ from the reference program's by a relative error of at most 0.000075.
Values sent between devices are 32-bit elements; how exact they have to be, the bound alone decides.
A program may use at most 128 MiB of HBM per device.

```python
import math
import jax
import jax.numpy as jnp
from jax import lax

TILE = 640
FINE = 1600
NROWS = 5120
NCOLS = 20480
FROWS = 12800
FCOLS = 51200
N_ROW = 8


def steps_of(own_key, extent, cuts, least, high):
    factor_of = 1.0
    for axis_at, parts in cuts:
        heights = jax.random.uniform(jax.random.fold_in(jax.random.fold_in(own_key, 6), axis_at), (parts,), jnp.float32, least / len(cuts), high / len(cuts))
        factor_of = factor_of * jnp.repeat(jnp.exp(heights), extent[axis_at] // parts).reshape((-1,) + (1,) * (len(extent) - 1 - axis_at))
    return factor_of


def scatter_about(own_key, dims, spread, bound, split=(), kind=jnp.bfloat16):
    array = spread * jax.random.normal(own_key, dims, jnp.float32)
    if split:
        array = array * steps_of(own_key, dims, split, -0.22, 0.18)
    return jnp.clip(array, -bound, bound).astype(kind)


def setup_inputs(seed: int = 0) -> dict:
    streams_of = jax.random.split(jax.random.key(seed), 3)
    level_set = scatter_about(streams_of[0], (FROWS, FCOLS), 8.0, 48.0, ((0, 8), (1, 32)), jnp.float32)
    dose_map = jnp.clip(jnp.exp(math.log(1.6) - 0.98082923 * jax.random.uniform(streams_of[1], (NROWS, NCOLS), jnp.float32) ** steps_of(streams_of[1], (NROWS, NCOLS), ((0, 256),), -0.2, 0.2)), 0.6, 1.6)
    return {"level_set": level_set, "dose_map": dose_map}


edge_width = 2.0
raw_taps = [math.exp(-0.5 * (offset - 4) ** 2) for offset in range(9)]
blur_taps = [raw_value / sum(raw_taps) for raw_value in raw_taps]


def tent_table(block_rows):
    centre = 2.5 * jnp.arange(block_rows, dtype=jnp.float32) + 0.75
    places = jnp.arange(block_rows * 5 // 2 + 2, dtype=jnp.float32) - 1.0
    distance = jnp.abs(places[None, :] - centre[:, None])
    return jnp.maximum(0.0, 1.0 - distance / 2.5) / 2.5


def resample_cols(field, tent):
    block_rows = tent.shape[0]
    window_len = tent.shape[1] - 2
    block_count = (field.shape[1] - 2) // window_len
    row_count = field.shape[0]
    leading = field[:, :block_count * window_len].reshape(row_count, block_count, window_len)
    trailing = field[:, 2:block_count * window_len + 2].reshape(row_count, block_count, window_len)[:, :, window_len - 2:]
    windows = jnp.concatenate([leading, trailing], axis=2)
    result = jnp.einsum('rbq,jq->rbj', windows, tent, precision=lax.Precision.HIGHEST)
    return result.reshape(row_count, block_count * block_rows)


def resample_rows(field, tent):
    block_rows = tent.shape[0]
    window_len = tent.shape[1] - 2
    block_count = (field.shape[0] - 2) // window_len
    col_count = field.shape[1]
    leading = field[:block_count * window_len].reshape(block_count, window_len, col_count)
    trailing = field[2:block_count * window_len + 2].reshape(block_count, window_len, col_count)[:, window_len - 2:]
    windows = jnp.concatenate([leading, trailing], axis=1)
    result = jnp.einsum('jq,bqc->bjc', tent, windows, precision=lax.Precision.HIGHEST)
    return result.reshape(block_count * block_rows, col_count)


def blur_rows(padded):
    length = padded.shape[0] - 8
    summed = blur_taps[0] * padded[0:length]
    for offset in range(1, 9):
        summed = summed + blur_taps[offset] * padded[offset:offset + length]
    return summed


def blur_cols(field):
    length = field.shape[-1]
    padded = jnp.pad(field, [(0, 0)] * (field.ndim - 1) + [(4, 4)])
    summed = blur_taps[0] * padded[..., 0:length]
    for offset in range(1, 9):
        summed = summed + blur_taps[offset] * padded[..., offset:offset + length]
    return summed


def reference(level_set, dose_map):
    tent = tent_table(math.gcd(TILE, 128))
    padded = jnp.pad(level_set, ((0, 0), (1, 1)))
    bands = padded.reshape(N_ROW, FINE, FCOLS + 2)
    colres = lax.map(lambda band_rows: resample_cols(band_rows, tent), bands).reshape(FROWS, NCOLS)
    colres = jnp.pad(colres, ((1, 1), (0, 0)))
    coarse = resample_rows(colres, tent)
    cover = jax.nn.sigmoid(coarse / edge_width)
    rowblur = blur_rows(jnp.pad(cover, ((4, 4), (0, 0))))
    blurred = blur_cols(rowblur)
    return dose_map * blurred
```

```python
import functools
import math

import jax
import jax.numpy as jnp
from jax import lax
from jax.experimental import pallas as pl
from jax.experimental.pallas import tpu as pltpu
from jax.sharding import PartitionSpec as P

F32, BF16 = jnp.float32, jnp.bfloat16
MESH = pl.DeviceIdType.MESH
RAW_TAPS = [math.exp(-0.5 * k * k) for k in range(5)]
TAPS = [t / (RAW_TAPS[0] + 2.0 * sum(RAW_TAPS[1:])) for t in RAW_TAPS]

FINE, TILE, STRIPE = 1600, 640, 20
TOP = 24
XROWS = TOP + FINE + 24
CROWS = 656
CHUNK = 208
LANES = 1664
BASES = (0, 256, 512, 896, 1152)
SLOT = 100
PART_A = 60


def row_groups(x_ref, group, out_ref, out_row):
    start = TOP - 20 + 40 * group
    for tile in range(LANES // 128):
        a = [x_ref[tile, pl.ds(start + s, 8, stride=5), :] for s in range(-1, 6)]
        even = 3.0 * a[0] + 7.0 * a[1] + 9.0 * a[2] + 5.0 * a[3] + a[4]
        odd = a[2] + 5.0 * a[3] + 9.0 * a[4] + 7.0 * a[5] + 3.0 * a[6]
        out_ref[tile, pl.ds(out_row, 8, stride=2), :] = even
        out_ref[tile, pl.ds(out_row + 1, 8, stride=2), :] = odd


def col_tile(rr_ref, count, w_ref, tile):
    first = BASES[tile] // 128
    rows = jnp.concatenate([rr_ref[first + t, 0:count, :] for t in range(4)], axis=1)
    hi = rows.astype(BF16)
    rest = rows - hi.astype(F32)
    mid = rest.astype(BF16)
    low = (rest - mid.astype(F32)).astype(BF16)
    w = w_ref[tile]
    dot = functools.partial(jnp.dot, preferred_element_type=F32)
    return dot(hi, w) + dot(mid, w) + dot(low, w)


def coverage(total):
    return 1.0 / (1.0 + jnp.exp(total * (-1.0 / 1250.0)))


def blur_block(cov_ref, d, tile):
    first = STRIPE * d + 4
    taps = [cov_ref[tile, pl.ds(first + k, STRIPE), :] for k in range(9)]
    total = TAPS[0] * taps[4]
    for k in range(1, 5):
        total = total + TAPS[k] * (taps[4 - k] + taps[4 + k])
    return total


def piece_a(cov_ref, send_ref, d):
    for t in range(3):
        send_ref[d, STRIPE * t : STRIPE * t + STRIPE, :] = blur_block(cov_ref, d, t + 1)


def piece_b(cov_ref, send_ref, d):
    for t in range(2):
        send_ref[d, PART_A + STRIPE * t : PART_A + STRIPE * t + STRIPE, :] = blur_block(cov_ref, d, 4 * t)


def tile_kernel(
    n_row, n_col, x_hbm, got_ref,
    x_in, x_ref, w_ref, rr_ref, cov_ref, send_ref, strip_ref, halo_out, halo_in,
    load_sem, row_send, row_recv, col_send, col_recv, send_sem, recv_sem, own_sem,
):
    row, col = lax.axis_index("row"), lax.axis_index("col")
    z, y, core = col // 8, lax.rem(col // 2, 4), lax.rem(col, 2)
    up, down, left, right = row > 0, row < n_row - 1, col > 0, col < n_col - 1

    def load(part):
        rows = pl.ds(400 * part, 400)
        return pltpu.make_async_copy(x_hbm.at[rows], x_in.at[rows], load_sem.at[part])

    for part in range(4):
        load(part).start()

    barrier = pltpu.get_barrier_semaphore()

    @pl.loop(1, n_col)
    def _(k):
        pl.semaphore_signal(barrier, 1, device_id=(row, lax.rem(col + k, n_col)), device_id_type=MESH)

    for there, other in ((up, row - 1), (down, row + 1)):
        @pl.when(there)
        def _(other=other):
            pl.semaphore_signal(barrier, 1, device_id=(other, col), device_id_type=MESH)

    k_at = lax.broadcasted_iota(jnp.int32, (512, 128), 0)
    n_at = lax.broadcasted_iota(jnp.int32, (512, 128), 1)
    for tile in range(5):
        far = jnp.abs(4 * k_at - 10 * n_at + (4 * BASES[tile] - 1280 * tile - 3))
        w_ref[tile] = jnp.maximum(10 - far, 0).astype(F32).astype(BF16)
    x_ref[12, TOP : TOP + FINE, 64:128] = jnp.zeros((FINE, 64), F32)
    x_ref[:, 0:8, :] = jnp.zeros((13, 8, 128), F32)
    x_ref[:, XROWS - 8 : XROWS, :] = jnp.zeros((13, 8, 128), F32)
    strip_ref[:, CROWS:768, :] = jnp.zeros((2, 768 - CROWS, 128), F32)
    halo_in[0, 8:128, :] = jnp.zeros((120, 768), F32)
    halo_in[1, 0:120, :] = jnp.zeros((120, 768), F32)

    @pl.when(jnp.logical_not(up))
    def _():
        x_ref[:, 8:24, :] = jnp.zeros((13, 16, 128), F32)

    @pl.when(jnp.logical_not(down))
    def _():
        x_ref[:, XROWS - 24 : XROWS - 8, :] = jnp.zeros((13, 16, 128), F32)

    @pl.when(jnp.logical_not(left))
    def _():
        halo_in[0, 0:8, :] = jnp.zeros((8, 768), F32)

    @pl.when(jnp.logical_not(right))
    def _():
        halo_in[1, 120:128, :] = jnp.zeros((8, 768), F32)

    for part in range(4):
        load(part).wait()

        @pl.loop(0, 10)
        def _(g, part=part):
            start = pl.multiple_of(400 * part + 40 * g, 8)
            for tile in range(12):
                x_ref[tile, pl.ds(TOP + start, 40), :] = x_in[pl.ds(start, 40), 128 * tile : 128 * tile + 128]
            x_ref[12, pl.ds(TOP + start, 40), 0:64] = x_in[pl.ds(start, 40), 1536:1600]

    @pl.loop(0, 3)
    def _(chunk):
        @pl.loop(0, 13)
        def _(g):
            row_groups(x_ref, 1 + 13 * chunk + g, rr_ref, 16 * g)

        at = pl.ds(pl.multiple_of(16 + CHUNK * chunk, 16), CHUNK)
        strip_ref[0, at, :] = rr_ref[0]
        strip_ref[1, at, :] = rr_ref[12]
        for tile in range(5):
            total = col_tile(rr_ref, CHUNK, w_ref, tile)
            cov_ref[tile, at, :] = total if tile in (0, 4) else coverage(total)

    @pl.loop(1, n_col - 1)
    def _(d):
        piece_a(cov_ref, send_ref, d)

    pl.semaphore_wait(barrier, n_col - 1 + up.astype(jnp.int32) + down.astype(jnp.int32))

    def row_halo(i):
        if i == 0:
            return pltpu.make_async_remote_copy(
                x_ref.at[:, pl.ds(TOP + FINE - 16, 16)], x_ref.at[:, pl.ds(TOP - 16, 16)],
                row_send.at[0], row_recv.at[0], device_id=(row + 1, col), device_id_type=MESH)
        return pltpu.make_async_remote_copy(
            x_ref.at[:, pl.ds(TOP, 16)], x_ref.at[:, pl.ds(TOP + FINE, 16)],
            row_send.at[1], row_recv.at[1], device_id=(row - 1, col), device_id_type=MESH)

    def col_halo(i):
        if i == 0:
            return pltpu.make_async_remote_copy(
                halo_out.at[0], halo_in.at[0, pl.ds(0, 8)],
                col_send.at[0], col_recv.at[0], device_id=(row, col + 1), device_id_type=MESH)
        return pltpu.make_async_remote_copy(
            halo_out.at[1], halo_in.at[1, pl.ds(120, 8)],
            col_send.at[1], col_recv.at[1], device_id=(row, col - 1), device_id_type=MESH)

    @pl.when(down)
    def _():
        row_halo(0).start()

    @pl.when(up)
    def _():
        row_halo(1).start()

    def piece(part, d, slot):
        rows = pl.ds(0, PART_A) if part == 0 else pl.ds(PART_A, SLOT - PART_A)
        return pltpu.make_async_remote_copy(
            send_ref.at[d, rows], got_ref.at[slot, rows],
            send_sem.at[part, d], recv_sem.at[part, slot], device_id=(row, d), device_id_type=MESH)

    def target(i):
        far = i < 24
        j = jnp.where(far, i // 3, i - 24)
        dz = jnp.where(far, 1 + lax.rem(2 * lax.rem(i, 3), 3), 0)
        return lax.rem(z + dz, 4) * 8 + lax.rem(y + j // 2, 4) * 2 + lax.rem(core + lax.rem(j, 2), 2)

    def inner(d):
        return jnp.logical_and(d > 0, d < n_col - 1)

    @pl.loop(0, n_col)
    def _(i):
        d = target(i)

        @pl.when(jnp.logical_and(inner(d), i != 24))
        def _():
            piece(0, d, col).start()

    @pl.when(up)
    def _():
        row_halo(0).wait_recv()

    @pl.when(down)
    def _():
        row_halo(1).wait_recv()

    row_groups(x_ref, 0, rr_ref, 0)
    row_groups(x_ref, 40, rr_ref, 16)
    strip_ref[0, 0:16, :] = rr_ref[0, 0:16, :]
    strip_ref[1, 0:16, :] = rr_ref[12, 0:16, :]
    strip_ref[0, CROWS - 16 : CROWS, :] = rr_ref[0, 16:32, :]
    strip_ref[1, CROWS - 16 : CROWS, :] = rr_ref[12, 16:32, :]

    sub = lax.broadcasted_iota(jnp.int32, (8, 768), 0)
    last = jnp.transpose(strip_ref[1])[63:64, :]
    halo_out[0] = jnp.where(sub == 0, 3.0 * last, 0.0)
    first = jnp.transpose(strip_ref[0])[0:1, :]
    halo_out[1] = jnp.where(sub == 7, 3.0 * first, 0.0)

    @pl.when(right)
    def _():
        col_halo(0).start()

    @pl.when(left)
    def _():
        col_halo(1).start()

    def in_window(i0, count):
        j = lax.broadcasted_iota(jnp.int32, (count, 128), 0) + (TILE * row + i0 - 8)
        return jnp.logical_and(j >= 0, j < TILE * n_row)

    for tile in range(5):
        total = col_tile(rr_ref, 32, w_ref, tile)
        for part, i0 in ((total[0:16], 0), (total[16:32], CROWS - 16)):
            if tile not in (0, 4):
                part = jnp.where(in_window(i0, 16), coverage(part), 0.0)
            cov_ref[tile, i0 : i0 + 16, :] = part

    for d in (0, n_col - 1):
        piece_a(cov_ref, send_ref, d)

        @pl.when(col != d)
        def _(d=d):
            piece(0, d, col).start()

    for side, there in ((0, left), (1, right)):
        @pl.when(there)
        def _(side=side):
            col_halo(side).wait_recv()

        extra = jnp.transpose(halo_in[side])
        total = cov_ref[4 * side] + extra[0:CROWS]
        cov_ref[4 * side] = jnp.where(in_window(0, CROWS), coverage(total), 0.0)

    @pl.loop(0, n_col)
    def _(i):
        d = target(i)
        piece_b(cov_ref, send_ref, d)

        @pl.when(i != 24)
        def _():
            piece(1, d, col).start()

    own = pltpu.make_async_copy(send_ref.at[col], got_ref.at[col], own_sem)
    own.start()

    @pl.when(down)
    def _():
        row_halo(0).wait_send()

    @pl.when(up)
    def _():
        row_halo(1).wait_send()

    @pl.when(right)
    def _():
        col_halo(0).wait_send()

    @pl.when(left)
    def _():
        col_halo(1).wait_send()

    own.wait()

    @pl.loop(0, n_col)
    def _(k):
        @pl.when(k != col)
        def _():
            for part in range(2):
                piece(part, k, k).wait_send()
                piece(part, k, k).wait_recv()


def exchange(level_set, n_row, n_col):
    any_space = pl.BlockSpec(memory_space=pl.ANY)
    return pl.pallas_call(
        functools.partial(tile_kernel, n_row, n_col),
        out_shape=jax.ShapeDtypeStruct((n_col, SLOT, 128), F32),
        in_specs=[any_space],
        out_specs=any_space,
        scratch_shapes=[
            pltpu.VMEM((FINE, FINE), F32),
            pltpu.VMEM((13, XROWS, 128), F32),
            pltpu.VMEM((5, 512, 128), BF16),
            pltpu.VMEM((13, CHUNK, 128), F32),
            pltpu.VMEM((5, CROWS, 128), F32),
            pltpu.VMEM((n_col, SLOT, 128), F32),
            pltpu.VMEM((2, 768, 128), F32),
            pltpu.VMEM((2, 8, 768), F32),
            pltpu.VMEM((2, 128, 768), F32),
            pltpu.SemaphoreType.DMA((4,)),
            pltpu.SemaphoreType.DMA((2,)),
            pltpu.SemaphoreType.DMA((2,)),
            pltpu.SemaphoreType.DMA((2,)),
            pltpu.SemaphoreType.DMA((2,)),
            pltpu.SemaphoreType.DMA((2, n_col)),
            pltpu.SemaphoreType.DMA((2, n_col)),
            pltpu.SemaphoreType.DMA,
        ],
        compiler_params=pltpu.CompilerParams(
            collective_id=0, has_side_effects=True, vmem_limit_bytes=48 << 20
        ),
        name="resample_exchange",
    )(level_set)


STEP = 4


def slot_rows(ref, at, tile):
    first = STRIPE * (tile - 1) if 0 < tile < 4 else PART_A + STRIPE * (tile // 4)
    return ref[at, first : first + STRIPE, :]


def finish_kernel(steps, prev_ref, cur_ref, next_ref, dose_ref, out_ref):
    step = pl.program_id(0)
    width = STEP * TILE
    before = jnp.where(step > 0, slot_rows(prev_ref, 0, 4), 0.0)
    after = jnp.where(step < steps - 1, slot_rows(next_ref, 0, 0), 0.0)
    field = jnp.concatenate(
        [before] + [slot_rows(cur_ref, s, t) for s in range(STEP) for t in range(5)] + [after],
        axis=1,
    )
    total = TAPS[0] * field
    for k in range(1, 5):
        total = total + TAPS[k] * (pltpu.roll(field, k, 1) + pltpu.roll(field, width + 256 - k, 1))
    out_ref[...] = dose_ref[...] * total[:, 128 : 128 + width]


def finish(got, dose_map, n_col):
    steps = n_col // STEP
    return pl.pallas_call(
        functools.partial(finish_kernel, steps),
        grid=(steps,),
        out_shape=jax.ShapeDtypeStruct(dose_map.shape, F32),
        in_specs=[
            pl.BlockSpec((1, SLOT, 128), lambda i: (jnp.maximum(STEP * i - 1, 0), 0, 0)),
            pl.BlockSpec((STEP, SLOT, 128), lambda i: (i, 0, 0)),
            pl.BlockSpec((1, SLOT, 128), lambda i: (jnp.minimum(STEP * i + STEP, n_col - 1), 0, 0)),
            pl.BlockSpec((STRIPE, STEP * TILE), lambda i: (0, i)),
        ],
        out_specs=pl.BlockSpec((STRIPE, STEP * TILE), lambda i: (0, i)),
        name="finish",
    )(got, got, got, dose_map)


def solution(mesh):
    n_row, n_col = mesh.shape["row"], mesh.shape["col"]

    def local(level_set, dose_map):
        return finish(exchange(level_set, n_row, n_col), dose_map, n_col)

    return jax.shard_map(
        local,
        mesh=mesh,
        in_specs=(P("row", "col"), P(("row", "col"), None)),
        out_specs=P(("row", "col"), None),
        check_vma=False,
    )
```

```python
import functools
import math

import jax
import jax.numpy as jnp
from jax import lax
from jax.experimental import pallas as pl
from jax.experimental.pallas import tpu as pltpu
from jax.sharding import PartitionSpec as P

F32, BF16 = jnp.float32, jnp.bfloat16
MESH = pl.DeviceIdType.MESH
RAW_TAPS = [math.exp(-0.5 * k * k) for k in range(5)]
TAPS = [t / (RAW_TAPS[0] + 2.0 * sum(RAW_TAPS[1:])) for t in RAW_TAPS]

FINE, TILE, STRIPE = 1600, 640, 20
TILES = 13
PART = 464
CHUNK = 176
CROWS = 656
HROWS = 768
BASES = (0, 256, 512, 896, 1152)
SLOT = 100
PART_A = 60


def to_tiles(src_ref, src_at, dst_ref, dst_at, count):
    for tile in range(TILES - 1):
        dst_ref[tile, pl.ds(dst_at, count), :] = src_ref[pl.ds(src_at, count), 128 * tile : 128 * tile + 128]
    dst_ref[12, pl.ds(dst_at, count), 0:64] = src_ref[pl.ds(src_at, count), 1536:1600]


def row_groups(x_ref, start, out_ref, out_row):
    for tile in range(TILES):
        a = [x_ref[tile, pl.ds(start + s, 8, stride=5), :] for s in range(-1, 6)]
        even = 3.0 * a[0] + 7.0 * a[1] + 9.0 * a[2] + 5.0 * a[3] + a[4]
        odd = a[2] + 5.0 * a[3] + 9.0 * a[4] + 7.0 * a[5] + 3.0 * a[6]
        out_ref[tile, pl.ds(out_row, 8, stride=2), :] = even
        out_ref[tile, pl.ds(out_row + 1, 8, stride=2), :] = odd


def dot(a, b):
    return jnp.dot(a, b, preferred_element_type=F32)


def tent_dot(rows, w):
    hi = rows.astype(BF16)
    rest = rows - hi.astype(F32)
    mid = rest.astype(BF16)
    low = (rest - mid.astype(F32)).astype(BF16)
    return dot(hi, w) + dot(mid, w) + dot(low, w)


def col_tile(rr_ref, count, w_ref, tile):
    first = BASES[tile] // 128
    return tent_dot(jnp.concatenate([rr_ref[first + t, 0:count, :] for t in range(4)], axis=1), w_ref[tile])


def coverage(total):
    return 1.0 / (1.0 + jnp.exp(total * (-1.0 / 1250.0)))


def halves(cover):
    hi = cover.astype(BF16)
    return hi, (cover - hi.astype(F32)).astype(BF16)


def col_blur(pieces, g_ref):
    hi = jnp.concatenate([p[0] for p in pieces], axis=1)
    low = jnp.concatenate([p[1] for p in pieces], axis=1)
    return dot(hi, g_ref[0]) + dot(low, g_ref[0]) + dot(hi, g_ref[1])


def row_blur(cb_ref, d, tile):
    first = STRIPE * d + 4
    taps = [cb_ref[tile, pl.ds(first + k, STRIPE), :] for k in range(9)]
    total = TAPS[0] * taps[4]
    for k in range(1, 5):
        total = total + TAPS[k] * (taps[4 - k] + taps[4 + k])
    return total


def piece_a(cb_ref, send_ref, d):
    for t in range(3):
        send_ref[d, STRIPE * t : STRIPE * t + STRIPE, :] = row_blur(cb_ref, d, t + 1)


def piece_b(cb_ref, send_ref, d):
    for t in range(2):
        send_ref[d, PART_A + STRIPE * t : PART_A + STRIPE * t + STRIPE, :] = row_blur(cb_ref, d, 4 * t)


def make_weights(w_ref, we_ref, g_ref):
    def tent(fine_col, coarse_col):
        return jnp.maximum(10 - jnp.abs(4 * fine_col - 10 * coarse_col - 3), 0)

    k = lax.broadcasted_iota(jnp.int32, (512, 128), 0)
    n = lax.broadcasted_iota(jnp.int32, (512, 128), 1)
    for tile in range(5):
        w_ref[tile] = tent(k + BASES[tile], n + 128 * tile).astype(F32).astype(BF16)

    k = lax.broadcasted_iota(jnp.int32, (128, 128), 0)
    n = lax.broadcasted_iota(jnp.int32, (128, 128), 1)
    beyond = jnp.where(n < 4, n + 640, n - 128)
    is_beyond = jnp.logical_or(n < 4, n >= 124)
    halo_col = jnp.where(k < 16, k - 16, k + 1584)
    is_halo = k < 32
    zero = jnp.zeros((128, 128), BF16)
    for part, (fine, use) in enumerate(((k, k >= 0), (k + 1536, k < 64), (halo_col, is_halo))):
        for out, (coarse, ok) in enumerate(((n, use), (n + 512, use), (beyond, jnp.logical_and(use, is_beyond)))):
            rows, cols = pl.ds(128 * part, 128), pl.ds(128 * out, 128)
            if part < 2 and out < 2:
                we_ref[rows, cols] = zero
            else:
                we_ref[rows, cols] = jnp.where(ok, tent(fine, coarse), 0).astype(F32).astype(BF16)

    k = lax.broadcasted_iota(jnp.int32, (384, 128), 0)
    n = lax.broadcasted_iota(jnp.int32, (384, 128), 1)
    off = jnp.abs(k - n - 128)
    g = jnp.zeros((384, 128), F32)
    for step in range(5):
        g = jnp.where(off == step, TAPS[step], g)
    hi, low = halves(g)
    g_ref[0] = hi
    g_ref[1] = low


def tile_kernel(
    n_row, n_col, x_hbm, dose_hbm, out_hbm,
    x_in, x_top, x_bot, x_ref, top_ref, bot_ref, w_ref, we_ref, g_ref, rr_ref, sum_ref, cov_ref, cb_ref,
    strip_ref, halo_out, halo_in, send_ref, got_ref, dose_ref, out_ref,
    load_sem, edge_sem, dose_sem, row_send, row_recv, col_send, col_recv, send_sem, recv_sem, own_sem, out_sem,
):
    row, col = lax.axis_index("row"), lax.axis_index("col")
    z, y, core = col // 8, lax.rem(col // 2, 4), lax.rem(col, 2)
    up, down, left, right = row > 0, row < n_row - 1, col > 0, col < n_col - 1

    def chunk_at(step):
        return lax.rem(z + jnp.where(step == 0, 2, jnp.where(step == 1, 1, jnp.where(step == 2, 3, 0))), 4)

    def load_start(c):
        return pl.multiple_of(jnp.clip(400 * c - 24, 0, FINE - PART), 8)

    def load(c):
        return pltpu.make_async_copy(x_hbm.at[pl.ds(load_start(c), PART)], x_in.at[c], load_sem.at[c])

    load(chunk_at(0)).start()
    edges = [
        pltpu.make_async_copy(x_hbm.at[pl.ds(0, 24)], x_top, edge_sem.at[0]),
        pltpu.make_async_copy(x_hbm.at[pl.ds(FINE - 24, 24)], x_bot, edge_sem.at[1]),
    ]
    for edge in edges:
        edge.start()
    for step in range(1, 4):
        load(chunk_at(step)).start()
    dose = pltpu.make_async_copy(dose_hbm, dose_ref, dose_sem)
    dose.start()

    top_ref[:, 0:8, :] = jnp.zeros((TILES, 8, 128), F32)
    bot_ref[:, 40:48, :] = jnp.zeros((TILES, 8, 128), F32)
    halo_in[32:128, :] = jnp.zeros((96, HROWS), F32)

    @pl.when(jnp.logical_not(up))
    def _():
        top_ref[:, 8:24, :] = jnp.zeros((TILES, 16, 128), F32)

    @pl.when(jnp.logical_not(down))
    def _():
        bot_ref[:, 24:40, :] = jnp.zeros((TILES, 16, 128), F32)

    @pl.when(jnp.logical_not(left))
    def _():
        halo_in[0:16, :] = jnp.zeros((16, HROWS), F32)

    @pl.when(jnp.logical_not(right))
    def _():
        halo_in[16:32, :] = jnp.zeros((16, HROWS), F32)

    barrier = pltpu.get_barrier_semaphore()

    @pl.loop(1, n_col)
    def _(k):
        pl.semaphore_signal(barrier, 1, device_id=(row, lax.rem(col + k, n_col)), device_id_type=MESH)

    for there, other in ((up, row - 1), (down, row + 1)):
        @pl.when(there)
        def _(other=other):
            pl.semaphore_signal(barrier, 1, device_id=(other, col), device_id_type=MESH)

    make_weights(w_ref, we_ref, g_ref)
    x_ref[12, :, 64:128] = jnp.zeros((PART, 64), F32)
    top_ref[12, 24:48, 64:128] = jnp.zeros((24, 64), F32)
    bot_ref[12, 0:24, 64:128] = jnp.zeros((24, 64), F32)
    strip_ref[0:2, CROWS:HROWS, :] = jnp.zeros((2, HROWS - CROWS, 128), F32)

    def row_halo(i):
        if i == 0:
            return pltpu.make_async_remote_copy(
                bot_ref.at[:, pl.ds(8, 16)], top_ref.at[:, pl.ds(8, 16)],
                row_send.at[0], row_recv.at[0], device_id=(row + 1, col), device_id_type=MESH)
        return pltpu.make_async_remote_copy(
            top_ref.at[:, pl.ds(24, 16)], bot_ref.at[:, pl.ds(24, 16)],
            row_send.at[1], row_recv.at[1], device_id=(row - 1, col), device_id_type=MESH)

    def col_halo(i):
        if i == 0:
            return pltpu.make_async_remote_copy(
                halo_out.at[0], halo_in.at[pl.ds(0, 16)],
                col_send.at[0], col_recv.at[0], device_id=(row, col + 1), device_id_type=MESH)
        return pltpu.make_async_remote_copy(
            halo_out.at[1], halo_in.at[pl.ds(16, 16)],
            col_send.at[1], col_recv.at[1], device_id=(row, col - 1), device_id_type=MESH)

    def piece(part, d, slot):
        rows = pl.ds(0, PART_A) if part == 0 else pl.ds(PART_A, SLOT - PART_A)
        return pltpu.make_async_remote_copy(
            send_ref.at[d, rows], got_ref.at[slot, rows],
            send_sem.at[part, d], recv_sem.at[part, slot], device_id=(row, d), device_id_type=MESH)

    def in_chunk(c, s):
        return 8 * c + lax.rem(y + s // 2, 4) * 2 + lax.rem(core + lax.rem(s, 2), 2)

    def resample(c):
        load(c).wait()
        base = load_start(c)

        @pl.loop(0, PART // 8)
        def _(g):
            at = pl.multiple_of(8 * g, 8)
            to_tiles(x_in.at[c], at, x_ref, at, 8)

        first = jnp.clip(10 * c, 1, 29)

        @pl.loop(0, 11)
        def _(g):
            row_groups(x_ref, 40 * (first + g) - 20 - base, rr_ref, 16 * g)

        at = pl.ds(16 * first, CHUNK)
        strip_ref[0, at, :] = rr_ref[0]
        strip_ref[1, at, :] = rr_ref[12]
        cover = []
        for tile in range(5):
            total = col_tile(rr_ref, CHUNK, w_ref, tile)
            if tile in (0, 4):
                sum_ref[tile // 4, at, :] = total
            total = coverage(total)
            if tile in (1, 3):
                cov_ref[tile // 2, at, :] = total
            cover.append(halves(total))
        for tile in range(1, 4):
            cb_ref[tile, at, :] = col_blur(cover[tile - 1 : tile + 2], g_ref)

    def send_a(c):
        @pl.loop(0, 8)
        def _(s):
            d = in_chunk(c, s)

            @pl.when(jnp.logical_and(d > 0, d < n_col - 1))
            def _():
                piece_a(cb_ref, send_ref, d)

                @pl.when(d != col)
                def _():
                    piece(0, d, col).start()

    @pl.loop(0, 4)
    def _(step):
        c = chunk_at(step)
        resample(c)

        @pl.when(step == 0)
        def _():
            for edge in edges:
                edge.wait()
            to_tiles(x_top, 0, top_ref, 24, 24)
            to_tiles(x_bot, 0, bot_ref, 0, 24)
            pl.semaphore_wait(barrier, n_col - 1 + up.astype(jnp.int32) + down.astype(jnp.int32))

            @pl.when(down)
            def _():
                row_halo(0).start()

            @pl.when(up)
            def _():
                row_halo(1).start()

        send_a(c)

    @pl.when(up)
    def _():
        row_halo(0).wait_recv()

    @pl.when(down)
    def _():
        row_halo(1).wait_recv()

    row_groups(top_ref, 4, rr_ref, 0)
    row_groups(bot_ref, 4, rr_ref, 16)
    ends = ((slice(0, 16), 0), (slice(16, 32), CROWS - 16))
    for part, i0 in ends:
        strip_ref[0, i0 : i0 + 16, :] = rr_ref[0, part, :]
        strip_ref[1, i0 : i0 + 16, :] = rr_ref[12, part, :]

    halo_out[0] = jnp.transpose(strip_ref[1])[48:64, :]
    halo_out[1] = jnp.transpose(strip_ref[0])[0:16, :]

    @pl.when(right)
    def _():
        col_halo(0).start()

    @pl.when(left)
    def _():
        col_halo(1).start()

    def in_window(i0, count):
        j = lax.broadcasted_iota(jnp.int32, (count, 128), 0) + (TILE * row + i0 - 8)
        return jnp.logical_and(j >= 0, j < TILE * n_row)

    cover = []
    end_rows = jnp.concatenate([in_window(0, 16), in_window(CROWS - 16, 16)], axis=0)
    for tile in range(5):
        total = col_tile(rr_ref, 32, w_ref, tile)
        if tile in (0, 4):
            for part, i0 in ends:
                sum_ref[tile // 4, i0 : i0 + 16, :] = total[part]
        total = jnp.where(end_rows, coverage(total), 0.0)
        if tile in (1, 3):
            for part, i0 in ends:
                cov_ref[tile // 2, i0 : i0 + 16, :] = total[part]
        cover.append(halves(total))
    for tile in range(1, 4):
        total = col_blur(cover[tile - 1 : tile + 2], g_ref)
        for part, i0 in ends:
            cb_ref[tile, i0 : i0 + 16, :] = total[part]

    for d in (0, n_col - 1):
        piece_a(cb_ref, send_ref, d)

        @pl.when(col != d)
        def _(d=d):
            piece(0, d, col).start()

    @pl.when(left)
    def _():
        col_halo(0).wait_recv()

    @pl.when(right)
    def _():
        col_halo(1).wait_recv()

    halo = jnp.transpose(halo_in[...])
    for part in range(HROWS // 128):
        strip_ref[2, 128 * part : 128 * part + 128, :] = halo[128 * part : 128 * part + 128]

    lane = lax.broadcasted_iota(jnp.int32, (CHUNK, 128), 1)

    @pl.loop(0, 4)
    def _(step):
        c = chunk_at(step)
        at = pl.ds(160 * c, CHUNK)
        extra = tent_dot(jnp.concatenate([strip_ref[k, at, :] for k in range(3)], axis=1), we_ref[...])
        inside = in_window(160 * c, CHUNK)
        first = jnp.where(inside, coverage(sum_ref[0, at, :] + extra[:, 0:128]), 0.0)
        last = jnp.where(inside, coverage(sum_ref[1, at, :] + extra[:, 128:256]), 0.0)
        held = jnp.logical_or(jnp.logical_and(right, lane < 4), jnp.logical_and(left, lane >= 124))
        beyond = jnp.where(jnp.logical_and(inside, held), coverage(extra[:, 256:384]), 0.0)
        beyond = halves(beyond)
        cb_ref[0, at, :] = col_blur([beyond, halves(first), halves(cov_ref[0, at, :])], g_ref)
        cb_ref[4, at, :] = col_blur([halves(cov_ref[1, at, :]), halves(last), beyond], g_ref)

        @pl.loop(0, 8)
        def _(s):
            d = in_chunk(c, s)
            piece_b(cb_ref, send_ref, d)

            @pl.when(d != col)
            def _():
                piece(1, d, col).start()

    own = pltpu.make_async_copy(send_ref.at[col], got_ref.at[col], own_sem)
    own.start()
    dose.wait()

    def write(c):
        lanes = pl.ds(pl.multiple_of(TILE * c, 128), TILE)
        return pltpu.make_async_copy(out_ref.at[:, lanes], out_hbm.at[:, lanes], out_sem.at[c])

    def finish(c):
        for place, tile in enumerate((1, 2, 3, 0, 4)):
            lanes = pl.ds(pl.multiple_of(TILE * c + 128 * tile, 128), 128)
            out_ref[:, lanes] = dose_ref[:, lanes] * got_ref[c, STRIPE * place : STRIPE * place + STRIPE, :]
        write(c).start()

    own.wait()
    finish(col)

    @pl.loop(1, n_col)
    def _(i):
        group = i // 8
        dz = jnp.where(group == 0, 0, jnp.where(group == 1, 2, jnp.where(group == 2, 1, 3)))
        s = lax.rem(i, 8)
        c = lax.rem(z + 4 - dz, 4) * 8 + lax.rem(y + 4 - s // 2, 4) * 2 + lax.rem(core + lax.rem(s, 2), 2)
        piece(0, c, c).wait_recv()
        piece(1, c, c).wait_recv()
        finish(c)

    @pl.when(down)
    def _():
        row_halo(0).wait_send()

    @pl.when(up)
    def _():
        row_halo(1).wait_send()

    @pl.when(right)
    def _():
        col_halo(0).wait_send()

    @pl.when(left)
    def _():
        col_halo(1).wait_send()

    @pl.loop(0, n_col)
    def _(k):
        @pl.when(k != col)
        def _():
            for part in range(2):
                piece(part, k, k).wait_send()

        write(k).wait()


def solution(mesh):
    n_row, n_col = mesh.shape["row"], mesh.shape["col"]
    any_space = pl.BlockSpec(memory_space=pl.ANY)

    def local(level_set, dose_map):
        return pl.pallas_call(
            functools.partial(tile_kernel, n_row, n_col),
            out_shape=jax.ShapeDtypeStruct(dose_map.shape, F32),
            in_specs=[any_space, any_space],
            out_specs=any_space,
            scratch_shapes=[
                pltpu.VMEM((4, PART, FINE), F32),
                pltpu.VMEM((24, FINE), F32),
                pltpu.VMEM((24, FINE), F32),
                pltpu.VMEM((TILES, PART, 128), F32),
                pltpu.VMEM((TILES, 48, 128), F32),
                pltpu.VMEM((TILES, 48, 128), F32),
                pltpu.VMEM((5, 512, 128), BF16),
                pltpu.VMEM((384, 384), BF16),
                pltpu.VMEM((2, 384, 128), BF16),
                pltpu.VMEM((TILES, CHUNK, 128), F32),
                pltpu.VMEM((2, CROWS, 128), F32),
                pltpu.VMEM((2, CROWS, 128), F32),
                pltpu.VMEM((5, CROWS, 128), F32),
                pltpu.VMEM((3, HROWS, 128), F32),
                pltpu.VMEM((2, 16, HROWS), F32),
                pltpu.VMEM((128, HROWS), F32),
                pltpu.VMEM((n_col, SLOT, 128), F32),
                pltpu.VMEM((n_col, SLOT, 128), F32),
                pltpu.VMEM(dose_map.shape, F32),
                pltpu.VMEM(dose_map.shape, F32),
                pltpu.SemaphoreType.DMA((4,)),
                pltpu.SemaphoreType.DMA((2,)),
                pltpu.SemaphoreType.DMA,
                pltpu.SemaphoreType.DMA((2,)),
                pltpu.SemaphoreType.DMA((2,)),
                pltpu.SemaphoreType.DMA((2,)),
                pltpu.SemaphoreType.DMA((2,)),
                pltpu.SemaphoreType.DMA((2, n_col)),
                pltpu.SemaphoreType.DMA((2, n_col)),
                pltpu.SemaphoreType.DMA,
                pltpu.SemaphoreType.DMA((n_col,)),
            ],
            compiler_params=pltpu.CompilerParams(
                collective_id=0, has_side_effects=True, vmem_limit_bytes=52 << 20
            ),
            name="resample_exchange",
        )(level_set, dose_map)

    return jax.shard_map(
        local,
        mesh=mesh,
        in_specs=(P("row", "col"), P(("row", "col"), None)),
        out_specs=P(("row", "col"), None),
        check_vma=False,
    )
```

```python
import functools
import math

import jax
import jax.numpy as jnp
from jax import lax
from jax.experimental import pallas as pl
from jax.experimental.pallas import tpu as pltpu
from jax.sharding import PartitionSpec as P

F32, BF16 = jnp.float32, jnp.bfloat16
MESH = pl.DeviceIdType.MESH
RAW_TAPS = [math.exp(-0.5 * k * k) for k in range(5)]
TAPS = [t / (RAW_TAPS[0] + 2.0 * sum(RAW_TAPS[1:])) for t in RAW_TAPS]

FINE, TILE, STRIPE = 1600, 640, 20
TILES = 13
PART = 464
CHUNK = 176
CROWS = 656
HROWS = 768
BASES = (0, 256, 512, 896, 1152)
SLOT = 100
PART_A = 60


def to_tiles(src_ref, src_at, dst_ref, dst_at, count):
    for tile in range(TILES - 1):
        dst_ref[tile, pl.ds(dst_at, count), :] = src_ref[pl.ds(src_at, count), 128 * tile : 128 * tile + 128]
    dst_ref[12, pl.ds(dst_at, count), 0:64] = src_ref[pl.ds(src_at, count), 1536:1600]


def row_group(x_ref, tile, start, out_ref, out_row):
    a = [x_ref[tile, pl.ds(start + s, 8, stride=5), :] for s in range(-1, 6)]
    even = 3.0 * a[0] + 7.0 * a[1] + 9.0 * a[2] + 5.0 * a[3] + a[4]
    odd = a[2] + 5.0 * a[3] + 9.0 * a[4] + 7.0 * a[5] + 3.0 * a[6]
    out_ref[tile, pl.ds(out_row, 8, stride=2), :] = even
    out_ref[tile, pl.ds(out_row + 1, 8, stride=2), :] = odd


def dot(a, b):
    return jnp.dot(a, b, preferred_element_type=F32)


def tent_dot(rows, w):
    hi = rows.astype(BF16)
    rest = rows - hi.astype(F32)
    mid = rest.astype(BF16)
    low = (rest - mid.astype(F32)).astype(BF16)
    return dot(hi, w) + dot(mid, w) + dot(low, w)


def col_tile(rr_ref, count, w_ref, tile):
    first = BASES[tile] // 128
    return tent_dot(jnp.concatenate([rr_ref[first + t, 0:count, :] for t in range(4)], axis=1), w_ref[tile])


def coverage(total):
    return 1.0 / (1.0 + jnp.exp(total * (-1.0 / 1250.0)))


def halves(cover):
    hi = cover.astype(BF16)
    return hi, (cover - hi.astype(F32)).astype(BF16)


def col_blur(pieces, g_ref):
    hi = jnp.concatenate([p[0] for p in pieces], axis=1)
    low = jnp.concatenate([p[1] for p in pieces], axis=1)
    return dot(hi, g_ref[0]) + dot(low, g_ref[0]) + dot(hi, g_ref[1])


def row_blur(cb_ref, d, tile):
    first = STRIPE * d + 4
    taps = [cb_ref[tile, pl.ds(first + k, STRIPE), :] for k in range(9)]
    total = TAPS[0] * taps[4]
    for k in range(1, 5):
        total = total + TAPS[k] * (taps[4 - k] + taps[4 + k])
    return total


def piece_a(cb_ref, send_ref, d):
    for t in range(3):
        send_ref[d, STRIPE * t : STRIPE * t + STRIPE, :] = row_blur(cb_ref, d, t + 1)


def piece_b(cb_ref, send_ref, d):
    for t in range(2):
        send_ref[d, PART_A + STRIPE * t : PART_A + STRIPE * t + STRIPE, :] = row_blur(cb_ref, d, 4 * t)


def make_weights(w_ref, we_ref, g_ref):
    def tent(fine_col, coarse_col):
        return jnp.maximum(10 - jnp.abs(4 * fine_col - 10 * coarse_col - 3), 0)

    k = lax.broadcasted_iota(jnp.int32, (512, 128), 0)
    n = lax.broadcasted_iota(jnp.int32, (512, 128), 1)
    for tile in range(5):
        w_ref[tile] = tent(k + BASES[tile], n + 128 * tile).astype(F32).astype(BF16)

    k = lax.broadcasted_iota(jnp.int32, (256, 128), 0)
    n = lax.broadcasted_iota(jnp.int32, (256, 128), 1)
    to_left = tent(jnp.where(k < 128, k, k + 1408), n - 1)
    to_right = tent(jnp.where(k < 128, k, k + 1408), n + 628)
    use = jnp.logical_and(n >= 8, n < 13)
    we_ref[...] = jnp.where(n < 5, to_left, jnp.where(use, to_right, 0)).astype(F32).astype(BF16)

    k = lax.broadcasted_iota(jnp.int32, (384, 128), 0)
    n = lax.broadcasted_iota(jnp.int32, (384, 128), 1)
    off = jnp.abs(k - n - 128)
    g = jnp.zeros((384, 128), F32)
    for step in range(5):
        g = jnp.where(off == step, TAPS[step], g)
    hi, low = halves(g)
    g_ref[0] = hi
    g_ref[1] = low


def row_groups(x_ref, start, out_ref, out_row):
    for tile in range(TILES):
        row_group(x_ref, tile, start, out_ref, out_row)


def tile_kernel(
    n_row, n_col, x_hbm, dose_hbm, out_hbm,
    x_in, x_ref, end_x_ref, side_x_ref, w_ref, we_ref, g_ref, rr_ref, sum_ref, cov_ref, cb_ref,
    strip_ref, own_ref, side_ref, side_out, side_in, end_ref, end_out, end_in,
    send_ref, got_ref, dose_ref, out_ref,
    load_sem, dose_sem, row_send, row_recv, col_send, col_recv, send_sem, recv_sem, own_sem, out_sem,
):
    row, col = lax.axis_index("row"), lax.axis_index("col")
    z, y, core = col // 8, lax.rem(col // 2, 4), lax.rem(col, 2)
    up, down, left, right = row > 0, row < n_row - 1, col > 0, col < n_col - 1

    def chunk_at(step):
        return lax.rem(z + jnp.where(step == 0, 2, jnp.where(step == 1, 1, jnp.where(step == 2, 3, 0))), 4)

    def load_start(c):
        return pl.multiple_of(jnp.clip(400 * c - 24, 0, FINE - PART), 8)

    def load(c):
        return pltpu.make_async_copy(x_hbm.at[pl.ds(load_start(c), PART)], x_in.at[c], load_sem.at[c])

    for step in range(4):
        load(chunk_at(step)).start()
    dose = pltpu.make_async_copy(dose_hbm, dose_ref, dose_sem)
    dose.start()

    side_in[...] = jnp.zeros(side_in.shape, F32)
    end_in[...] = jnp.zeros(end_in.shape, F32)

    barrier = pltpu.get_barrier_semaphore()

    @pl.loop(1, n_col)
    def _(k):
        pl.semaphore_signal(barrier, 1, device_id=(row, lax.rem(col + k, n_col)), device_id_type=MESH)

    for there, other in ((up, row - 1), (down, row + 1)):
        @pl.when(there)
        def _(other=other):
            pl.semaphore_signal(barrier, 1, device_id=(other, col), device_id_type=MESH)

    make_weights(w_ref, we_ref, g_ref)
    x_ref[12, :, 64:128] = jnp.zeros((PART, 64), F32)
    end_x_ref[0, :, 0:24, :] = jnp.zeros((TILES, 24, 128), F32)
    end_x_ref[1, :, 24:48, :] = jnp.zeros((TILES, 24, 128), F32)
    end_x_ref[:, 12, :, 64:128] = jnp.zeros((2, 48, 64), F32)
    side_x_ref[:, 0:24, :] = jnp.zeros((2, 24, 128), F32)
    side_x_ref[:, FINE + 24 : FINE + 48, :] = jnp.zeros((2, 24, 128), F32)
    side_x_ref[1, 24 : FINE + 24, 64:128] = jnp.zeros((FINE, 64), F32)
    own_ref[CROWS:HROWS, :] = jnp.zeros((HROWS - CROWS, 128), F32)

    def row_halo(i):
        return pltpu.make_async_remote_copy(
            end_out.at[i], end_in.at[i],
            row_send.at[i], row_recv.at[i], device_id=(row + 1 - 2 * i, col), device_id_type=MESH)

    def col_halo(i):
        return pltpu.make_async_remote_copy(
            side_out.at[i], side_in.at[i],
            col_send.at[i], col_recv.at[i], device_id=(row, col + 1 - 2 * i), device_id_type=MESH)

    def piece(part, d, slot):
        rows = pl.ds(0, PART_A) if part == 0 else pl.ds(PART_A, SLOT - PART_A)
        return pltpu.make_async_remote_copy(
            send_ref.at[d, rows], got_ref.at[slot, rows],
            send_sem.at[part, d], recv_sem.at[part, slot], device_id=(row, d), device_id_type=MESH)

    def in_chunk(c, s):
        return 8 * c + lax.rem(y + s // 2, 4) * 2 + lax.rem(core + lax.rem(s, 2), 2)

    def resample(c):
        base = load_start(c)

        @pl.loop(0, PART // 8)
        def _(g):
            at = pl.multiple_of(8 * g, 8)
            to_tiles(x_in.at[c], at, x_ref, at, 8)

        first = jnp.clip(10 * c, 1, 29)

        @pl.loop(0, 11)
        def _(g):
            row_groups(x_ref, 40 * (first + g) - 20 - base, rr_ref, 16 * g)

        at = pl.ds(16 * first, CHUNK)
        cover = []
        for tile in range(5):
            total = col_tile(rr_ref, CHUNK, w_ref, tile)
            if tile in (0, 4):
                sum_ref[tile // 4, at, :] = total
            total = coverage(total)
            if tile in (1, 3):
                cov_ref[tile // 2, at, :] = total
            cover.append(halves(total))
        for tile in range(1, 4):
            cb_ref[tile, at, :] = col_blur(cover[tile - 1 : tile + 2], g_ref)

    def send_a(c):
        @pl.loop(0, 8)
        def _(s):
            d = in_chunk(c, s)

            @pl.when(jnp.logical_and(d > 0, d < n_col - 1))
            def _():
                piece_a(cb_ref, send_ref, d)

                @pl.when(d != col)
                def _():
                    piece(0, d, col).start()

    def sides():
        for step in range(1, 4):
            load(chunk_at(step)).wait()
        for c in range(4):
            skip = 24 if 0 < c < 3 else 64 if c == 3 else 0

            @pl.loop(0, 10)
            def _(g, c=c, skip=skip):
                source = pl.ds(pl.multiple_of(skip + 40 * g, 8), 40)
                target = pl.ds(pl.multiple_of(24 + 400 * c + 40 * g, 8), 40)
                side_x_ref[0, target, :] = x_in[c, source, 0:128]
                side_x_ref[1, target, 0:64] = x_in[c, source, 1536:1600]

        @pl.loop(0, CROWS // 16)
        def _(g):
            for side in range(2):
                row_group(side_x_ref, side, 4 + 40 * g, strip_ref, 16 * g)

        own_ref[0:CROWS, :] = tent_dot(jnp.concatenate([strip_ref[0], strip_ref[1]], axis=1), we_ref[...])
        for part in range(HROWS // 128):
            columns = jnp.transpose(own_ref[128 * part : 128 * part + 128, :])
            side_out[0, part] = columns[8:13, :]
            side_out[1, part] = columns[0:5, :]

        @pl.when(right)
        def _():
            col_halo(0).start()

        @pl.when(left)
        def _():
            col_halo(1).start()

    @pl.loop(0, 4)
    def _(step):
        c = chunk_at(step)

        @pl.when(step == 0)
        def _():
            load(c).wait()

        resample(c)

        @pl.when(step == 0)
        def _():
            pl.semaphore_wait(barrier, n_col - 1 + up.astype(jnp.int32) + down.astype(jnp.int32))

        send_a(c)

        @pl.when(step == 0)
        def _():
            sides()

    to_tiles(x_in.at[0], 0, end_x_ref.at[0], 24, 24)
    to_tiles(x_in.at[3], PART - 24, end_x_ref.at[1], 0, 24)
    for end in range(2):
        row_groups(end_x_ref.at[end], 4, rr_ref, 16 * end)
    for tile in range(5):
        end_ref[tile] = col_tile(rr_ref, 32, w_ref, tile)

    @pl.when(left)
    def _():
        col_halo(0).wait_recv()

    @pl.when(right)
    def _():
        col_halo(1).wait_recv()

    for part in range(HROWS // 128):
        held = jnp.concatenate(
            [side_in[0, part], jnp.zeros((3, 128), F32), side_in[1, part], jnp.zeros((115, 128), F32)], axis=0)
        side_ref[128 * part : 128 * part + 128, :] = jnp.transpose(held)

    def edges(at, count):
        lane = lax.broadcasted_iota(jnp.int32, (count, 128), 1)
        got, own = side_ref[at, :], own_ref[at, :]
        low, high = pltpu.roll(got, 124, 1), pltpu.roll(got, 119, 1)
        beyond = jnp.where(lane >= 124, low, jnp.where(lane < 4, high, 0.0))
        beyond = beyond + jnp.where(lane == 127, pltpu.roll(own, 127, 1), 0.0)
        beyond = beyond + jnp.where(lane == 0, pltpu.roll(own, 116, 1), 0.0)
        return jnp.where(lane == 0, low, 0.0), jnp.where(lane == 127, high, 0.0), beyond

    def held_lanes(count):
        lane = lax.broadcasted_iota(jnp.int32, (count, 128), 1)
        return jnp.logical_or(jnp.logical_and(right, lane < 4), jnp.logical_and(left, lane >= 124))

    ends = ((0, 0), (16, CROWS - 16))
    for i, i0 in ends:
        first, last, beyond = edges(pl.ds(i0, 16), 16)
        end_ref[0, i : i + 16, :] = end_ref[0, i : i + 16, :] + first
        end_ref[4, i : i + 16, :] = end_ref[4, i : i + 16, :] + last
        end_ref[5, i : i + 16, :] = beyond
    end_out[0] = end_ref[:, 20:25, :]
    end_out[1] = end_ref[:, 7:12, :]

    @pl.when(down)
    def _():
        row_halo(0).start()

    @pl.when(up)
    def _():
        row_halo(1).start()

    def send_b(d):
        piece_b(cb_ref, send_ref, d)

        @pl.when(d != col)
        def _():
            piece(1, d, col).start()

    @pl.loop(0, 4)
    def _(step):
        c = chunk_at(step)
        at = pl.ds(pl.multiple_of(16 * jnp.clip(10 * c, 1, 29), 16), CHUNK)
        first, last, beyond = edges(at, CHUNK)
        first = halves(coverage(sum_ref[0, at, :] + first))
        last = halves(coverage(sum_ref[1, at, :] + last))
        beyond = halves(jnp.where(held_lanes(CHUNK), coverage(beyond), 0.0))
        cb_ref[0, at, :] = col_blur([beyond, first, halves(cov_ref[0, at, :])], g_ref)
        cb_ref[4, at, :] = col_blur([halves(cov_ref[1, at, :]), last, beyond], g_ref)

        @pl.loop(0, 8)
        def _(s):
            d = in_chunk(c, s)

            @pl.when(jnp.logical_and(d > 0, d < n_col - 1))
            def _():
                send_b(d)

    @pl.when(up)
    def _():
        row_halo(0).wait_recv()

    @pl.when(down)
    def _():
        row_halo(1).wait_recv()

    def in_window(i0):
        j = lax.broadcasted_iota(jnp.int32, (16, 128), 0) + (TILE * row + i0 - 8)
        return jnp.logical_and(j >= 0, j < TILE * n_row)

    inside = jnp.concatenate([in_window(i0) for _, i0 in ends], axis=0)
    cover = []
    for tile in range(6):
        end_ref[tile, 4:9, :] = end_ref[tile, 4:9, :] + end_in[0, tile]
        end_ref[tile, 23:28, :] = end_ref[tile, 23:28, :] + end_in[1, tile]
        keep = inside if tile < 5 else jnp.logical_and(inside, held_lanes(32))
        cover.append(halves(jnp.where(keep, coverage(end_ref[tile]), 0.0)))
    cover = [cover[5]] + cover
    for tile in range(5):
        total = col_blur(cover[tile : tile + 3], g_ref)
        for i, i0 in ends:
            cb_ref[tile, i0 : i0 + 16, :] = total[i : i + 16]

    for d in (0, n_col - 1):
        piece_a(cb_ref, send_ref, d)

        @pl.when(col != d)
        def _(d=d):
            piece(0, d, col).start()

        send_b(d)

    own = pltpu.make_async_copy(send_ref.at[col], got_ref.at[col], own_sem)
    own.start()
    dose.wait()

    def write(c):
        lanes = pl.ds(pl.multiple_of(TILE * c, 128), TILE)
        return pltpu.make_async_copy(out_ref.at[:, lanes], out_hbm.at[:, lanes], out_sem.at[c])

    def finish(c):
        for place, tile in enumerate((1, 2, 3, 0, 4)):
            lanes = pl.ds(pl.multiple_of(TILE * c + 128 * tile, 128), 128)
            out_ref[:, lanes] = dose_ref[:, lanes] * got_ref[c, STRIPE * place : STRIPE * place + STRIPE, :]
        write(c).start()

    own.wait()
    finish(col)

    @pl.loop(1, n_col)
    def _(i):
        group = i // 8
        dz = jnp.where(group == 0, 0, jnp.where(group == 1, 2, jnp.where(group == 2, 1, 3)))
        s = lax.rem(i, 8)
        c = lax.rem(z + 4 - dz, 4) * 8 + lax.rem(y + 4 - s // 2, 4) * 2 + lax.rem(core + lax.rem(s, 2), 2)
        piece(0, c, c).wait_recv()
        piece(1, c, c).wait_recv()
        finish(c)

    @pl.when(down)
    def _():
        row_halo(0).wait_send()

    @pl.when(up)
    def _():
        row_halo(1).wait_send()

    @pl.when(right)
    def _():
        col_halo(0).wait_send()

    @pl.when(left)
    def _():
        col_halo(1).wait_send()

    @pl.loop(0, n_col)
    def _(k):
        @pl.when(k != col)
        def _():
            for part in range(2):
                piece(part, k, k).wait_send()

        write(k).wait()


def solution(mesh):
    n_row, n_col = mesh.shape["row"], mesh.shape["col"]
    any_space = pl.BlockSpec(memory_space=pl.ANY)

    def local(level_set, dose_map):
        return pl.pallas_call(
            functools.partial(tile_kernel, n_row, n_col),
            out_shape=jax.ShapeDtypeStruct(dose_map.shape, F32),
            in_specs=[any_space, any_space],
            out_specs=any_space,
            scratch_shapes=[
                pltpu.VMEM((4, PART, FINE), F32),
                pltpu.VMEM((TILES, PART, 128), F32),
                pltpu.VMEM((2, TILES, 48, 128), F32),
                pltpu.VMEM((2, FINE + 48, 128), F32),
                pltpu.VMEM((5, 512, 128), BF16),
                pltpu.VMEM((256, 128), BF16),
                pltpu.VMEM((2, 384, 128), BF16),
                pltpu.VMEM((TILES, CHUNK, 128), F32),
                pltpu.VMEM((2, CROWS, 128), F32),
                pltpu.VMEM((2, CROWS, 128), F32),
                pltpu.VMEM((5, CROWS, 128), F32),
                pltpu.VMEM((2, CROWS, 128), F32),
                pltpu.VMEM((HROWS, 128), F32),
                pltpu.VMEM((HROWS, 128), F32),
                pltpu.VMEM((2, HROWS // 128, 5, 128), F32),
                pltpu.VMEM((2, HROWS // 128, 5, 128), F32),
                pltpu.VMEM((6, 32, 128), F32),
                pltpu.VMEM((2, 6, 5, 128), F32),
                pltpu.VMEM((2, 6, 5, 128), F32),
                pltpu.VMEM((n_col, SLOT, 128), F32),
                pltpu.VMEM((n_col, SLOT, 128), F32),
                pltpu.VMEM(dose_map.shape, F32),
                pltpu.VMEM(dose_map.shape, F32),
                pltpu.SemaphoreType.DMA((4,)),
                pltpu.SemaphoreType.DMA,
                pltpu.SemaphoreType.DMA((2,)),
                pltpu.SemaphoreType.DMA((2,)),
                pltpu.SemaphoreType.DMA((2,)),
                pltpu.SemaphoreType.DMA((2,)),
                pltpu.SemaphoreType.DMA((2, n_col)),
                pltpu.SemaphoreType.DMA((2, n_col)),
                pltpu.SemaphoreType.DMA,
                pltpu.SemaphoreType.DMA((n_col,)),
            ],
            compiler_params=pltpu.CompilerParams(
                collective_id=0, has_side_effects=True, vmem_limit_bytes=52 << 20
            ),
            name="resample_exchange",
        )(level_set, dose_map)

    return jax.shard_map(
        local,
        mesh=mesh,
        in_specs=(P("row", "col"), P(("row", "col"), None)),
        out_specs=P(("row", "col"), None),
        check_vma=False,
    )
```

```python
import functools
import math

import jax
import jax.numpy as jnp
from jax import lax
from jax.experimental import pallas as pl
from jax.experimental.pallas import tpu as pltpu
from jax.sharding import PartitionSpec as P

F32, BF16 = jnp.float32, jnp.bfloat16
MESH = pl.DeviceIdType.MESH
RAW_TAPS = [math.exp(-0.5 * k * k) for k in range(5)]
TAPS = [t / (RAW_TAPS[0] + 2.0 * sum(RAW_TAPS[1:])) for t in RAW_TAPS]

FINE, TILE, STRIPE = 1600, 640, 20
TILES = 13
PART = 264
UNIT = 96
CROWS = 656
HROWS = 768
BASES = (0, 256, 512, 896, 1152)
SLOT = 100
PART_A = 60


def to_tiles(src_ref, src_at, dst_ref, dst_at, count):
    for tile in range(TILES - 1):
        dst_ref[tile, pl.ds(dst_at, count), :] = src_ref[pl.ds(src_at, count), 128 * tile : 128 * tile + 128]
    dst_ref[12, pl.ds(dst_at, count), 0:64] = src_ref[pl.ds(src_at, count), 1536:1600]


def row_group(x_ref, tile, start, out_ref, out_row):
    a = [x_ref[tile, pl.ds(start + s, 8, stride=5), :] for s in range(-1, 6)]
    even = 3.0 * a[0] + 7.0 * a[1] + 9.0 * a[2] + 5.0 * a[3] + a[4]
    odd = a[2] + 5.0 * a[3] + 9.0 * a[4] + 7.0 * a[5] + 3.0 * a[6]
    out_ref[tile, pl.ds(out_row, 8, stride=2), :] = even
    out_ref[tile, pl.ds(out_row + 1, 8, stride=2), :] = odd


def dot(a, b):
    return jnp.dot(a, b, preferred_element_type=F32)


def tent_dot(rows, w):
    hi = rows.astype(BF16)
    rest = rows - hi.astype(F32)
    mid = rest.astype(BF16)
    low = (rest - mid.astype(F32)).astype(BF16)
    return dot(hi, w) + dot(mid, w) + dot(low, w)


def col_tile(rr_ref, count, w_ref, tile):
    first = BASES[tile] // 128
    return tent_dot(jnp.concatenate([rr_ref[first + t, 0:count, :] for t in range(4)], axis=1), w_ref[tile])


def coverage(total):
    return 1.0 / (1.0 + jnp.exp(total * (-1.0 / 1250.0)))


def halves(cover):
    hi = cover.astype(BF16)
    return hi, (cover - hi.astype(F32)).astype(BF16)


def col_blur(pieces, g_ref):
    hi = jnp.concatenate([p[0] for p in pieces], axis=1)
    low = jnp.concatenate([p[1] for p in pieces], axis=1)
    return dot(hi, g_ref[0]) + dot(low, g_ref[0]) + dot(hi, g_ref[1])


def row_blur(cb_ref, d, tile):
    first = STRIPE * d + 4
    taps = [cb_ref[tile, pl.ds(first + k, STRIPE), :] for k in range(9)]
    total = TAPS[0] * taps[4]
    for k in range(1, 5):
        total = total + TAPS[k] * (taps[4 - k] + taps[4 + k])
    return total


def piece_a(cb_ref, send_ref, d):
    for t in range(3):
        send_ref[d, STRIPE * t : STRIPE * t + STRIPE, :] = row_blur(cb_ref, d, t + 1)


def piece_b(cb_ref, send_ref, d):
    for t in range(2):
        send_ref[d, PART_A + STRIPE * t : PART_A + STRIPE * t + STRIPE, :] = row_blur(cb_ref, d, 4 * t)


def make_weights(w_ref, we_ref, g_ref):
    def tent(fine_col, coarse_col):
        return jnp.maximum(10 - jnp.abs(4 * fine_col - 10 * coarse_col - 3), 0)

    k = lax.broadcasted_iota(jnp.int32, (512, 128), 0)
    n = lax.broadcasted_iota(jnp.int32, (512, 128), 1)
    for tile in range(5):
        w_ref[tile] = tent(k + BASES[tile], n + 128 * tile).astype(F32).astype(BF16)

    k = lax.broadcasted_iota(jnp.int32, (256, 128), 0)
    n = lax.broadcasted_iota(jnp.int32, (256, 128), 1)
    to_left = tent(jnp.where(k < 128, k, k + 1408), n - 1)
    to_right = tent(jnp.where(k < 128, k, k + 1408), n + 628)
    use = jnp.logical_and(n >= 8, n < 13)
    we_ref[...] = jnp.where(n < 5, to_left, jnp.where(use, to_right, 0)).astype(F32).astype(BF16)

    k = lax.broadcasted_iota(jnp.int32, (384, 128), 0)
    n = lax.broadcasted_iota(jnp.int32, (384, 128), 1)
    off = jnp.abs(k - n - 128)
    g = jnp.zeros((384, 128), F32)
    for step in range(5):
        g = jnp.where(off == step, TAPS[step], g)
    hi, low = halves(g)
    g_ref[0] = hi
    g_ref[1] = low


def row_groups(x_ref, start, out_ref, out_row):
    for tile in range(TILES):
        row_group(x_ref, tile, start, out_ref, out_row)


def tile_kernel(
    n_row, n_col, x_hbm, dose_hbm, out_ref,
    x_in, x_ends, x_ref, end_x_ref, side_x_ref, w_ref, we_ref, g_ref, rr_ref, sum_ref, cov_ref, cb_ref,
    strip_ref, own_ref, side_ref, side_out, side_in, end_ref, end_out, end_in,
    corner_out, corner_in, send_ref, got_ref, dose_ref,
    load_sem, end_sem, dose_sem, row_send, row_recv, corner_send, corner_recv, col_send, col_recv, send_sem, recv_sem, own_sem,
):
    row, col = lax.axis_index("row"), lax.axis_index("col")
    z, y, core = col // 8, lax.rem(col // 2, 4), lax.rem(col, 2)
    up, down, left, right = row > 0, row < n_row - 1, col > 0, col < n_col - 1

    def pick(step, values):
        out = values[0]
        for k, value in enumerate(values[1:], 1):
            out = jnp.where(step == k, value, out)
        return out

    def unit_at(step):
        c = lax.rem(z + pick(step, (2, 2, 1, 3, 1, 3, 0, 0)), 4)
        return 2 * c + lax.rem(y // 2 + pick(step, (0, 1, 0, 0, 1, 1, 0, 1)), 2)

    def load_start(u):
        return pl.multiple_of(jnp.clip(200 * u - 24, 0, FINE - PART), 8)

    def load(u):
        return pltpu.make_async_copy(x_hbm.at[pl.ds(load_start(u), PART)], x_in.at[u], load_sem.at[u])

    end_loads = [
        pltpu.make_async_copy(x_hbm.at[pl.ds(at, 24)], x_ends.at[i], end_sem.at[i]) for i, at in enumerate((0, FINE - 24))
    ]
    for end_load in end_loads:
        end_load.start()
    for step in range(8):
        load(unit_at(step)).start()
    dose = pltpu.make_async_copy(dose_hbm, dose_ref, dose_sem)
    dose.start()

    side_in[...] = jnp.zeros(side_in.shape, F32)
    end_in[...] = jnp.zeros(end_in.shape, F32)
    corner_in[...] = jnp.zeros(corner_in.shape, F32)

    barrier = pltpu.get_barrier_semaphore()

    @pl.loop(1, n_col)
    def _(k):
        pl.semaphore_signal(barrier, 1, device_id=(row, lax.rem(col + k, n_col)), device_id_type=MESH)

    around = [
        (jnp.logical_and(dv, dh) if dh is not None else dv, row + v, col + h)
        for dv, v in ((up, -1), (down, 1))
        for dh, h in ((None, 0), (left, -1), (right, 1))
    ]
    for there, other_row, other_col in around:
        @pl.when(there)
        def _(other_row=other_row, other_col=other_col):
            pl.semaphore_signal(barrier, 1, device_id=(other_row, other_col), device_id_type=MESH)

    make_weights(w_ref, we_ref, g_ref)
    x_ref[12, :, 64:128] = jnp.zeros((PART, 64), F32)
    end_x_ref[0, :, 0:24, :] = jnp.zeros((TILES, 24, 128), F32)
    end_x_ref[1, :, 24:48, :] = jnp.zeros((TILES, 24, 128), F32)
    end_x_ref[:, 12, :, 64:128] = jnp.zeros((2, 48, 64), F32)
    side_x_ref[:, 0:24, :] = jnp.zeros((2, 24, 128), F32)
    side_x_ref[:, FINE + 24 : FINE + 48, :] = jnp.zeros((2, 24, 128), F32)
    side_x_ref[1, 24 : FINE + 24, 64:128] = jnp.zeros((FINE, 64), F32)
    own_ref[CROWS:HROWS, :] = jnp.zeros((HROWS - CROWS, 128), F32)

    def row_halo(i):
        return pltpu.make_async_remote_copy(
            end_out.at[i], end_in.at[i],
            row_send.at[i], row_recv.at[i], device_id=(row + 1 - 2 * i, col), device_id_type=MESH)

    corners = [(v, h, jnp.logical_and(dv, dh)) for v, dv in ((0, down), (1, up)) for h, dh in ((0, right), (1, left))]
    corners_in = [(v, h, jnp.logical_and(dv, dh)) for v, dv in ((0, up), (1, down)) for h, dh in ((0, left), (1, right))]

    def corner(v, h):
        return pltpu.make_async_remote_copy(
            corner_out.at[v], corner_in.at[v, h],
            corner_send.at[v, h], corner_recv.at[v, h],
            device_id=(row + 1 - 2 * v, col + 1 - 2 * h), device_id_type=MESH)

    def col_halo(i):
        return pltpu.make_async_remote_copy(
            side_out.at[i], side_in.at[i],
            col_send.at[i], col_recv.at[i], device_id=(row, col + 1 - 2 * i), device_id_type=MESH)

    def piece(part, d, slot):
        rows = pl.ds(0, PART_A) if part == 0 else pl.ds(PART_A, SLOT - PART_A)
        return pltpu.make_async_remote_copy(
            send_ref.at[d, rows], got_ref.at[slot, rows],
            send_sem.at[part], recv_sem.at[slot], device_id=(row, d), device_id_type=MESH)

    def stripe(u, s):
        return 4 * u + lax.rem(y + s // 2, 2) * 2 + lax.rem(core + lax.rem(s, 2), 2)

    def first_row(u):
        return pl.multiple_of(16 * jnp.clip(5 * u, 1, 34), 16)

    def resample(u):
        base = load_start(u)

        @pl.loop(0, PART // 24)
        def _(g):
            at = pl.multiple_of(24 * g, 8)
            to_tiles(x_in.at[u], at, x_ref, at, 24)

        first = first_row(u)

        @pl.loop(0, UNIT // 16)
        def _(g):
            row_groups(x_ref, 40 * (first // 16 + g) - 20 - base, rr_ref, 16 * g)

        at = pl.ds(first, UNIT)
        cover = []
        for tile in range(5):
            total = col_tile(rr_ref, UNIT, w_ref, tile)
            if tile in (0, 4):
                sum_ref[tile // 4, at, :] = total
            total = coverage(total)
            if tile in (1, 3):
                cov_ref[tile // 2, at, :] = total
            cover.append(halves(total))
        for tile in range(1, 4):
            cb_ref[tile, at, :] = col_blur(cover[tile - 1 : tile + 2], g_ref)

    def send_a(u, end):
        @pl.loop(0, 4)
        def _(s):
            d = stripe(u, s)
            is_end = jnp.logical_or(d == 0, d == n_col - 1)

            @pl.when(is_end == end)
            def _():
                piece_a(cb_ref, send_ref, d)

                @pl.when(d != col)
                def _():
                    piece(0, d, col).start()

            if end:
                piece_b(cb_ref, send_ref, d)

                @pl.when(d != col)
                def _():
                    piece(1, d, col).start()

    def lanes_of(count):
        return lax.broadcasted_iota(jnp.int32, (count, 128), 1)

    def beyond_own(own):
        lane = lanes_of(own.shape[0])
        return jnp.where(lane == 127, pltpu.roll(own, 127, 1), jnp.where(lane == 0, pltpu.roll(own, 116, 1), 0.0))

    def ends_own():
        for i in range(2):
            end_loads[i].wait()
            to_tiles(x_ends.at[i], 0, end_x_ref.at[i], 24 - 24 * i, 24)
            row_groups(end_x_ref.at[i], 4, rr_ref, 16 * i)
        for tile in range(5):
            end_ref[tile] = col_tile(rr_ref, 32, w_ref, tile)
        own = tent_dot(jnp.concatenate([rr_ref[0, 0:32, :], rr_ref[12, 0:32, :]], axis=1), we_ref[...])
        end_ref[5] = beyond_own(own)
        end_out[0] = end_ref[:, 20:25, :]
        end_out[1] = end_ref[:, 7:12, :]
        corner_out[0] = own[20:25]
        corner_out[1] = own[7:12]

    def send_ends():
        @pl.when(down)
        def _():
            row_halo(0).start()

        @pl.when(up)
        def _():
            row_halo(1).start()

        for v, h, there in corners:
            @pl.when(there)
            def _(v=v, h=h):
                corner(v, h).start()

    def sides():
        for step in range(1, 8):
            load(unit_at(step)).wait()

        @pl.loop(0, 8)
        def _(u):
            for g in range(5):
                source = pl.ds(pl.multiple_of(200 * u - load_start(u) + 40 * g, 8), 40)
                target = pl.ds(pl.multiple_of(24 + 200 * u + 40 * g, 8), 40)
                side_x_ref[0, target, :] = x_in[u, source, 0:128]
                side_x_ref[1, target, 0:64] = x_in[u, source, 1536:1600]

        @pl.loop(0, CROWS // 16)
        def _(g):
            for side in range(2):
                row_group(side_x_ref, side, 4 + 40 * g, strip_ref, 16 * g)

        own_ref[0:CROWS, :] = tent_dot(jnp.concatenate([strip_ref[0], strip_ref[1]], axis=1), we_ref[...])
        for part in range(HROWS // 128):
            columns = jnp.transpose(own_ref[128 * part : 128 * part + 128, :])
            side_out[0, part] = columns[8:13, :]
            side_out[1, part] = columns[0:5, :]

        @pl.when(right)
        def _():
            col_halo(0).start()

        @pl.when(left)
        def _():
            col_halo(1).start()

    ends = ((0, 0), (16, CROWS - 16))

    def in_window(i0):
        j = lax.broadcasted_iota(jnp.int32, (16, 128), 0) + (TILE * row + i0 - 8)
        return jnp.logical_and(j >= 0, j < TILE * n_row)

    def ends_a():
        @pl.when(up)
        def _():
            row_halo(0).wait_recv()

        @pl.when(down)
        def _():
            row_halo(1).wait_recv()

        inside = jnp.concatenate([in_window(i0) for _, i0 in ends], axis=0)
        cover = []
        for tile in range(6):
            end_ref[tile, 4:9, :] = end_ref[tile, 4:9, :] + end_in[0, tile]
            end_ref[tile, 23:28, :] = end_ref[tile, 23:28, :] + end_in[1, tile]
            if tile < 5:
                cover.append(halves(jnp.where(inside, coverage(end_ref[tile]), 0.0)))
        for tile in range(1, 4):
            total = col_blur(cover[tile - 1 : tile + 2], g_ref)
            for i, i0 in ends:
                cb_ref[tile, i0 : i0 + 16, :] = total[i : i + 16]

    ends_own()

    @pl.loop(0, 8)
    def _(step):
        u = unit_at(step)

        @pl.when(step == 0)
        def _():
            load(u).wait()

        resample(u)

        @pl.when(step == 0)
        def _():
            near = n_col - 1
            for there, _, _ in around:
                near = near + there.astype(jnp.int32)
            pl.semaphore_wait(barrier, near)
            send_ends()

        send_a(u, False)

        @pl.when(step == 0)
        def _():
            sides()

    ends_a()

    @pl.when(left)
    def _():
        col_halo(0).wait_recv()

    @pl.when(right)
    def _():
        col_halo(1).wait_recv()

    for part in range(HROWS // 128):
        held = jnp.concatenate(
            [side_in[0, part], jnp.zeros((3, 128), F32), side_in[1, part], jnp.zeros((115, 128), F32)], axis=0)
        side_ref[128 * part : 128 * part + 128, :] = jnp.transpose(held)

    def edges(at, count):
        lane, got = lanes_of(count), side_ref[at, :]
        low, high = pltpu.roll(got, 124, 1), pltpu.roll(got, 119, 1)
        beyond = jnp.where(lane >= 124, low, jnp.where(lane < 4, high, 0.0))
        return jnp.where(lane == 0, low, 0.0), jnp.where(lane == 127, high, 0.0), beyond

    def held_lanes(count):
        lane = lanes_of(count)
        return jnp.logical_or(jnp.logical_and(right, lane < 4), jnp.logical_and(left, lane >= 124))

    def blur_sides(at, count, first, last, beyond):
        first, last = halves(first), halves(last)
        beyond = halves(jnp.where(held_lanes(count), beyond, 0.0))
        return (
            col_blur([beyond, first, halves(cov_ref[0, at, :])], g_ref),
            col_blur([halves(cov_ref[1, at, :]), last, beyond], g_ref),
        )

    for v, h, there in corners_in:
        @pl.when(there)
        def _(v=v, h=h):
            corner(v, h).wait_recv()

    lane = lanes_of(5)
    for v, (i, i0) in enumerate(ends):
        first, last, beyond = edges(pl.ds(i0, 16), 16)
        end_ref[0, i : i + 16, :] = end_ref[0, i : i + 16, :] + first
        end_ref[4, i : i + 16, :] = end_ref[4, i : i + 16, :] + last
        end_ref[5, i : i + 16, :] = end_ref[5, i : i + 16, :] + beyond
        low, high = pltpu.roll(corner_in[v, 0], 116, 1), pltpu.roll(corner_in[v, 1], 127, 1)
        rows = slice(4, 9) if v == 0 else slice(23, 28)
        end_ref[0, rows, :] = end_ref[0, rows, :] + jnp.where(lane == 0, low, 0.0)
        end_ref[4, rows, :] = end_ref[4, rows, :] + jnp.where(lane == 127, high, 0.0)
        end_ref[5, rows, :] = end_ref[5, rows, :] + jnp.where(lane >= 124, low, jnp.where(lane < 4, high, 0.0))

    for i, i0 in ends:
        inside = in_window(i0)
        at, part = pl.ds(i0, 16), slice(i, i + 16)
        for k, tile in ((0, 1), (1, 3)):
            cov_ref[k, at, :] = jnp.where(inside, coverage(end_ref[tile, part, :]), 0.0)
        first, last, beyond = (jnp.where(inside, coverage(end_ref[tile, part, :]), 0.0) for tile in (0, 4, 5))
        cb_ref[0, at, :], cb_ref[4, at, :] = blur_sides(at, 16, first, last, beyond)

    @pl.loop(0, 8)
    def _(step):
        u = unit_at(step)
        at = pl.ds(first_row(u), UNIT)
        first, last, beyond = edges(at, UNIT)
        first = coverage(sum_ref[0, at, :] + first)
        last = coverage(sum_ref[1, at, :] + last)
        beyond = coverage(beyond + beyond_own(own_ref[at, :]))
        cb_ref[0, at, :], cb_ref[4, at, :] = blur_sides(at, UNIT, first, last, beyond)

        send_a(u, True)

    own = pltpu.make_async_copy(send_ref.at[col], got_ref.at[col], own_sem)
    own.start()
    dose.wait()

    def finish(c):
        for place, tile in enumerate((1, 2, 3, 0, 4)):
            lanes = pl.ds(pl.multiple_of(TILE * c + 128 * tile, 128), 128)
            out_ref[:, lanes] = dose_ref[:, lanes] * got_ref[c, STRIPE * place : STRIPE * place + STRIPE, :]

    own.wait()

    @pl.loop(0, 4)
    def _(i):
        dz = jnp.where(i == 0, 0, jnp.where(i == 1, 2, jnp.where(i == 2, 1, 3)))
        group = lax.rem(z + 4 - dz, 4)

        @pl.loop(0, 8)
        def _(s):
            c = group * 8 + lax.rem(y + 4 - s // 2, 4) * 2 + lax.rem(core + lax.rem(s, 2), 2)

            @pl.when(c != col)
            def _():
                pltpu.make_async_copy(send_ref.at[c], got_ref.at[c], recv_sem.at[c]).wait()

            finish(c)

    @pl.when(down)
    def _():
        row_halo(0).wait_send()

    @pl.when(up)
    def _():
        row_halo(1).wait_send()

    for v, h, there in corners:
        @pl.when(there)
        def _(v=v, h=h):
            corner(v, h).wait_send()

    @pl.when(right)
    def _():
        col_halo(0).wait_send()

    @pl.when(left)
    def _():
        col_halo(1).wait_send()

    for part, rows in enumerate((PART_A, SLOT - PART_A)):
        sent = send_ref.at[pl.ds(0, n_col - 1), pl.ds(0, rows)]
        pltpu.make_async_copy(sent, sent, send_sem.at[part]).wait()


def solution(mesh):
    n_row, n_col = mesh.shape["row"], mesh.shape["col"]
    any_space = pl.BlockSpec(memory_space=pl.ANY)

    def local(level_set, dose_map):
        return pl.pallas_call(
            functools.partial(tile_kernel, n_row, n_col),
            out_shape=jax.ShapeDtypeStruct(dose_map.shape, F32),
            in_specs=[any_space, any_space],
            out_specs=pl.BlockSpec(memory_space=pltpu.VMEM),
            scratch_shapes=[
                pltpu.VMEM((8, PART, FINE), F32),
                pltpu.VMEM((2, 24, FINE), F32),
                pltpu.VMEM((TILES, PART, 128), F32),
                pltpu.VMEM((2, TILES, 48, 128), F32),
                pltpu.VMEM((2, FINE + 48, 128), F32),
                pltpu.VMEM((5, 512, 128), BF16),
                pltpu.VMEM((256, 128), BF16),
                pltpu.VMEM((2, 384, 128), BF16),
                pltpu.VMEM((TILES, UNIT, 128), F32),
                pltpu.VMEM((2, CROWS, 128), F32),
                pltpu.VMEM((2, CROWS, 128), F32),
                pltpu.VMEM((5, CROWS, 128), F32),
                pltpu.VMEM((2, CROWS, 128), F32),
                pltpu.VMEM((HROWS, 128), F32),
                pltpu.VMEM((HROWS, 128), F32),
                pltpu.VMEM((2, HROWS // 128, 5, 128), F32),
                pltpu.VMEM((2, HROWS // 128, 5, 128), F32),
                pltpu.VMEM((6, 32, 128), F32),
                pltpu.VMEM((2, 6, 5, 128), F32),
                pltpu.VMEM((2, 6, 5, 128), F32),
                pltpu.VMEM((2, 5, 128), F32),
                pltpu.VMEM((2, 2, 5, 128), F32),
                pltpu.VMEM((n_col, SLOT, 128), F32),
                pltpu.VMEM((n_col, SLOT, 128), F32),
                pltpu.VMEM(dose_map.shape, F32),
                pltpu.SemaphoreType.DMA((8,)),
                pltpu.SemaphoreType.DMA((2,)),
                pltpu.SemaphoreType.DMA,
                pltpu.SemaphoreType.DMA((2,)),
                pltpu.SemaphoreType.DMA((2,)),
                pltpu.SemaphoreType.DMA((2, 2)),
                pltpu.SemaphoreType.DMA((2, 2)),
                pltpu.SemaphoreType.DMA((2,)),
                pltpu.SemaphoreType.DMA((2,)),
                pltpu.SemaphoreType.DMA((2,)),
                pltpu.SemaphoreType.DMA((n_col,)),
                pltpu.SemaphoreType.DMA,
            ],
            compiler_params=pltpu.CompilerParams(
                collective_id=0, has_side_effects=True, vmem_limit_bytes=52 << 20
            ),
            name="resample_exchange",
        )(level_set, dose_map)

    return jax.shard_map(
        local,
        mesh=mesh,
        in_specs=(P("row", "col"), P(("row", "col"), None)),
        out_specs=P(("row", "col"), None),
        check_vma=False,
    )
```

```python
import functools
import math

import jax
import jax.numpy as jnp
from jax import lax
from jax.experimental import pallas as pl
from jax.experimental.pallas import tpu as pltpu
from jax.sharding import PartitionSpec as P

F32, BF16 = jnp.float32, jnp.bfloat16
MESH = pl.DeviceIdType.MESH
RAW_TAPS = [math.exp(-0.5 * k * k) for k in range(5)]
TAPS = [t / (RAW_TAPS[0] + 2.0 * sum(RAW_TAPS[1:])) for t in RAW_TAPS]

FINE, TILE, STRIPE = 1600, 640, 20
TILES = 13
PART = 264
UNIT = 96
CROWS = 656
HROWS = 768
BASES = (0, 256, 512, 896, 1152)
SLOT = 100
PART_A = 60


def to_tiles(src_ref, src_at, dst_ref, dst_at, count):
    for tile in range(TILES - 1):
        dst_ref[tile, pl.ds(dst_at, count), :] = src_ref[pl.ds(src_at, count), 128 * tile : 128 * tile + 128]
    dst_ref[12, pl.ds(dst_at, count), 0:64] = src_ref[pl.ds(src_at, count), 1536:1600]


def row_group(x_ref, tile, start, out_ref, out_row):
    a = [x_ref[tile, pl.ds(start + s, 8, stride=5), :] for s in range(-1, 6)]
    even = 3.0 * a[0] + 7.0 * a[1] + 9.0 * a[2] + 5.0 * a[3] + a[4]
    odd = a[2] + 5.0 * a[3] + 9.0 * a[4] + 7.0 * a[5] + 3.0 * a[6]
    out_ref[tile, pl.ds(out_row, 8, stride=2), :] = even
    out_ref[tile, pl.ds(out_row + 1, 8, stride=2), :] = odd


def dot(a, b):
    return jnp.dot(a, b, preferred_element_type=F32)


def tent_dot(rows, w):
    hi = rows.astype(BF16)
    rest = rows - hi.astype(F32)
    mid = rest.astype(BF16)
    low = (rest - mid.astype(F32)).astype(BF16)
    return dot(hi, w) + dot(mid, w) + dot(low, w)


def col_tile(rr_ref, count, w_ref, tile):
    first = BASES[tile] // 128
    return tent_dot(jnp.concatenate([rr_ref[first + t, 0:count, :] for t in range(4)], axis=1), w_ref[tile])


def coverage(total):
    return 1.0 / (1.0 + jnp.exp(total * (-1.0 / 1250.0)))


def halves(cover):
    hi = cover.astype(BF16)
    return hi, (cover - hi.astype(F32)).astype(BF16)


def col_blur(pieces, g_ref):
    hi = jnp.concatenate([p[0] for p in pieces], axis=1)
    low = jnp.concatenate([p[1] for p in pieces], axis=1)
    return dot(hi, g_ref[0]) + dot(low, g_ref[0]) + dot(hi, g_ref[1])


def row_blur(cb_ref, d, tile):
    first = STRIPE * d + 4
    taps = [cb_ref[tile, pl.ds(first + k, STRIPE), :] for k in range(9)]
    total = TAPS[0] * taps[4]
    for k in range(1, 5):
        total = total + TAPS[k] * (taps[4 - k] + taps[4 + k])
    return total


def piece_a(cb_ref, send_ref, d):
    for t in range(3):
        send_ref[d, STRIPE * t : STRIPE * t + STRIPE, :] = row_blur(cb_ref, d, t + 1)


def piece_b(cb_ref, send_ref, d):
    for t in range(2):
        send_ref[d, PART_A + STRIPE * t : PART_A + STRIPE * t + STRIPE, :] = row_blur(cb_ref, d, 4 * t)


def make_weights(w_ref, we_ref, g_ref):
    def tent(fine_col, coarse_col):
        return jnp.maximum(10 - jnp.abs(4 * fine_col - 10 * coarse_col - 3), 0)

    k = lax.broadcasted_iota(jnp.int32, (512, 128), 0)
    n = lax.broadcasted_iota(jnp.int32, (512, 128), 1)
    for tile in range(5):
        w_ref[tile] = tent(k + BASES[tile], n + 128 * tile).astype(F32).astype(BF16)

    k = lax.broadcasted_iota(jnp.int32, (256, 128), 0)
    n = lax.broadcasted_iota(jnp.int32, (256, 128), 1)
    to_left = tent(jnp.where(k < 128, k, k + 1408), n - 1)
    to_right = tent(jnp.where(k < 128, k, k + 1408), n + 628)
    use = jnp.logical_and(n >= 8, n < 13)
    we_ref[...] = jnp.where(n < 5, to_left, jnp.where(use, to_right, 0)).astype(F32).astype(BF16)

    k = lax.broadcasted_iota(jnp.int32, (384, 128), 0)
    n = lax.broadcasted_iota(jnp.int32, (384, 128), 1)
    off = jnp.abs(k - n - 128)
    g = jnp.zeros((384, 128), F32)
    for step in range(5):
        g = jnp.where(off == step, TAPS[step], g)
    hi, low = halves(g)
    g_ref[0] = hi
    g_ref[1] = low


def row_groups(x_ref, start, out_ref, out_row):
    for tile in range(TILES):
        row_group(x_ref, tile, start, out_ref, out_row)


def tile_kernel(
    n_row, n_col, x_hbm, dose_hbm, out_ref,
    x_in, x_ends, x_ref, end_x_ref, side_x_ref, w_ref, we_ref, g_ref, rr_ref, sum_ref, cov_ref, cb_ref,
    strip_ref, own_ref, side_ref, side_out, side_in, end_ref, end_out, end_in,
    corner_out, corner_in, send_ref, got_ref, dose_ref,
    load_sem, end_sem, dose_sem, row_send, row_recv, corner_send, corner_recv, col_send, col_recv, send_sem, recv_sem, own_sem,
):
    row, col = lax.axis_index("row"), lax.axis_index("col")
    z, y, core = col // 8, lax.rem(col // 2, 4), lax.rem(col, 2)
    up, down, left, right = row > 0, row < n_row - 1, col > 0, col < n_col - 1

    def pick(step, values):
        out = values[0]
        for k, value in enumerate(values[1:], 1):
            out = jnp.where(step == k, value, out)
        return out

    def unit_at(step):
        c = lax.rem(z + pick(step, (2, 2, 1, 3, 1, 3, 0, 0)), 4)
        return 2 * c + lax.rem(y // 2 + pick(step, (0, 1, 0, 0, 1, 1, 0, 1)), 2)

    def load_start(u):
        return pl.multiple_of(jnp.clip(200 * u - 24, 0, FINE - PART), 8)

    def load(u):
        return pltpu.make_async_copy(x_hbm.at[pl.ds(load_start(u), PART)], x_in.at[u], load_sem.at[u])

    end_loads = [
        pltpu.make_async_copy(x_hbm.at[pl.ds(at, 24)], x_ends.at[i], end_sem.at[i]) for i, at in enumerate((0, FINE - 24))
    ]
    for end_load in end_loads:
        end_load.start()
    load(unit_at(0)).start()

    side_in[...] = jnp.zeros(side_in.shape, F32)
    end_in[...] = jnp.zeros(end_in.shape, F32)
    corner_in[...] = jnp.zeros(corner_in.shape, F32)

    barrier = pltpu.get_barrier_semaphore()

    @pl.loop(1, n_col)
    def _(k):
        pl.semaphore_signal(barrier, 1, device_id=(row, lax.rem(col + k, n_col)), device_id_type=MESH)

    around = [
        (jnp.logical_and(dv, dh) if dh is not None else dv, row + v, col + h)
        for dv, v in ((up, -1), (down, 1))
        for dh, h in ((None, 0), (left, -1), (right, 1))
    ]
    for there, other_row, other_col in around:
        @pl.when(there)
        def _(other_row=other_row, other_col=other_col):
            pl.semaphore_signal(barrier, 1, device_id=(other_row, other_col), device_id_type=MESH)

    for step in range(1, 8):
        load(unit_at(step)).start()
    dose = pltpu.make_async_copy(dose_hbm, dose_ref, dose_sem)
    dose.start()
    make_weights(w_ref, we_ref, g_ref)
    x_ref[12, :, 64:128] = jnp.zeros((PART, 64), F32)
    end_x_ref[0, :, 0:24, :] = jnp.zeros((TILES, 24, 128), F32)
    end_x_ref[1, :, 24:48, :] = jnp.zeros((TILES, 24, 128), F32)
    end_x_ref[:, 12, :, 64:128] = jnp.zeros((2, 48, 64), F32)
    side_x_ref[:, 0:24, :] = jnp.zeros((2, 24, 128), F32)
    side_x_ref[:, FINE + 24 : FINE + 48, :] = jnp.zeros((2, 24, 128), F32)
    side_x_ref[1, 24 : FINE + 24, 64:128] = jnp.zeros((FINE, 64), F32)
    own_ref[CROWS:HROWS, :] = jnp.zeros((HROWS - CROWS, 128), F32)

    def row_halo(i):
        return pltpu.make_async_remote_copy(
            end_out.at[i], end_in.at[i],
            row_send.at[i], row_recv.at[i], device_id=(row + 1 - 2 * i, col), device_id_type=MESH)

    corners = [(v, h, jnp.logical_and(dv, dh)) for v, dv in ((0, down), (1, up)) for h, dh in ((0, right), (1, left))]
    corners_in = [(v, h, jnp.logical_and(dv, dh)) for v, dv in ((0, up), (1, down)) for h, dh in ((0, left), (1, right))]

    def corner(v, h):
        return pltpu.make_async_remote_copy(
            corner_out.at[v], corner_in.at[v, h],
            corner_send.at[v, h], corner_recv.at[v, h],
            device_id=(row + 1 - 2 * v, col + 1 - 2 * h), device_id_type=MESH)

    def col_halo(i):
        return pltpu.make_async_remote_copy(
            side_out.at[i], side_in.at[i],
            col_send.at[i], col_recv.at[i], device_id=(row, col + 1 - 2 * i), device_id_type=MESH)

    def piece(part, d, slot):
        rows = pl.ds(0, PART_A) if part == 0 else pl.ds(PART_A, SLOT - PART_A)
        return pltpu.make_async_remote_copy(
            send_ref.at[d, rows], got_ref.at[slot, rows],
            send_sem.at[part], recv_sem.at[slot // 8], device_id=(row, d), device_id_type=MESH)

    def stripe(u, s):
        return 4 * u + lax.rem(y + s // 2, 2) * 2 + lax.rem(core + lax.rem(s, 2), 2)

    def first_row(u):
        return pl.multiple_of(16 * jnp.clip(5 * u, 1, 34), 16)

    def resample(u):
        base = load_start(u)

        @pl.loop(0, PART // 24)
        def _(g):
            at = pl.multiple_of(24 * g, 8)
            to_tiles(x_in.at[u], at, x_ref, at, 24)

        first = first_row(u)

        @pl.loop(0, UNIT // 16)
        def _(g):
            row_groups(x_ref, 40 * (first // 16 + g) - 20 - base, rr_ref, 16 * g)

        at = pl.ds(first, UNIT)
        cover = []
        for tile in range(5):
            total = col_tile(rr_ref, UNIT, w_ref, tile)
            if tile in (0, 4):
                sum_ref[tile // 4, at, :] = total
            total = coverage(total)
            if tile in (1, 3):
                cov_ref[tile // 2, at, :] = total
            cover.append(halves(total))
        for tile in range(1, 4):
            cb_ref[tile, at, :] = col_blur(cover[tile - 1 : tile + 2], g_ref)

    def send_a(u, end):
        @pl.loop(0, 4)
        def _(s):
            d = stripe(u, s)
            is_end = jnp.logical_or(d == 0, d == n_col - 1)

            @pl.when(is_end == end)
            def _():
                piece_a(cb_ref, send_ref, d)

                @pl.when(d != col)
                def _():
                    piece(0, d, col).start()

            if end:
                piece_b(cb_ref, send_ref, d)

                @pl.when(d != col)
                def _():
                    piece(1, d, col).start()

    def lanes_of(count):
        return lax.broadcasted_iota(jnp.int32, (count, 128), 1)

    def beyond_own(own):
        lane = lanes_of(own.shape[0])
        return jnp.where(lane == 127, pltpu.roll(own, 127, 1), jnp.where(lane == 0, pltpu.roll(own, 116, 1), 0.0))

    def ends_own():
        for i in range(2):
            end_loads[i].wait()
            to_tiles(x_ends.at[i], 0, end_x_ref.at[i], 24 - 24 * i, 24)
            row_groups(end_x_ref.at[i], 4, rr_ref, 16 * i)
        for tile in range(5):
            end_ref[tile] = col_tile(rr_ref, 32, w_ref, tile)
        own = tent_dot(jnp.concatenate([rr_ref[0, 0:32, :], rr_ref[12, 0:32, :]], axis=1), we_ref[...])
        end_ref[5] = beyond_own(own)
        end_out[0] = end_ref[:, 20:25, :]
        end_out[1] = end_ref[:, 7:12, :]
        corner_out[0] = own[20:25]
        corner_out[1] = own[7:12]

    def send_ends():
        @pl.when(down)
        def _():
            row_halo(0).start()

        @pl.when(up)
        def _():
            row_halo(1).start()

        for v, h, there in corners:
            @pl.when(there)
            def _(v=v, h=h):
                corner(v, h).start()

    def sides():
        for step in range(1, 8):
            load(unit_at(step)).wait()

        @pl.loop(0, 8)
        def _(u):
            for g in range(5):
                source = pl.ds(pl.multiple_of(200 * u - load_start(u) + 40 * g, 8), 40)
                target = pl.ds(pl.multiple_of(24 + 200 * u + 40 * g, 8), 40)
                side_x_ref[0, target, :] = x_in[u, source, 0:128]
                side_x_ref[1, target, 0:64] = x_in[u, source, 1536:1600]

        @pl.loop(0, CROWS // 16)
        def _(g):
            for side in range(2):
                row_group(side_x_ref, side, 4 + 40 * g, strip_ref, 16 * g)

        own_ref[0:CROWS, :] = tent_dot(jnp.concatenate([strip_ref[0], strip_ref[1]], axis=1), we_ref[...])
        for part in range(HROWS // 128):
            columns = jnp.transpose(own_ref[128 * part : 128 * part + 128, :])
            side_out[0, part] = columns[8:13, :]
            side_out[1, part] = columns[0:5, :]

        @pl.when(right)
        def _():
            col_halo(0).start()

        @pl.when(left)
        def _():
            col_halo(1).start()

    ends = ((0, 0), (16, CROWS - 16))

    def in_window(i0):
        j = lax.broadcasted_iota(jnp.int32, (16, 128), 0) + (TILE * row + i0 - 8)
        return jnp.logical_and(j >= 0, j < TILE * n_row)

    def ends_a():
        @pl.when(up)
        def _():
            row_halo(0).wait_recv()

        @pl.when(down)
        def _():
            row_halo(1).wait_recv()

        inside = jnp.concatenate([in_window(i0) for _, i0 in ends], axis=0)
        cover = []
        for tile in range(6):
            end_ref[tile, 4:9, :] = end_ref[tile, 4:9, :] + end_in[0, tile]
            end_ref[tile, 23:28, :] = end_ref[tile, 23:28, :] + end_in[1, tile]
            if tile < 5:
                cover.append(halves(jnp.where(inside, coverage(end_ref[tile]), 0.0)))
        for tile in range(1, 4):
            total = col_blur(cover[tile - 1 : tile + 2], g_ref)
            for i, i0 in ends:
                cb_ref[tile, i0 : i0 + 16, :] = total[i : i + 16]

    ends_own()

    @pl.loop(0, 8)
    def _(step):
        u = unit_at(step)

        @pl.when(step == 0)
        def _():
            load(u).wait()

        resample(u)

        @pl.when(step == 0)
        def _():
            near = n_col - 1
            for there, _, _ in around:
                near = near + there.astype(jnp.int32)
            pl.semaphore_wait(barrier, near)
            send_ends()

        send_a(u, False)

        @pl.when(step == 0)
        def _():
            sides()

    ends_a()

    @pl.when(left)
    def _():
        col_halo(0).wait_recv()

    @pl.when(right)
    def _():
        col_halo(1).wait_recv()

    for part in range(HROWS // 128):
        held = jnp.concatenate(
            [side_in[0, part], jnp.zeros((3, 128), F32), side_in[1, part], jnp.zeros((115, 128), F32)], axis=0)
        side_ref[128 * part : 128 * part + 128, :] = jnp.transpose(held)

    def edges(at, count):
        lane, got = lanes_of(count), side_ref[at, :]
        low, high = pltpu.roll(got, 124, 1), pltpu.roll(got, 119, 1)
        beyond = jnp.where(lane >= 124, low, jnp.where(lane < 4, high, 0.0))
        return jnp.where(lane == 0, low, 0.0), jnp.where(lane == 127, high, 0.0), beyond

    def held_lanes(count):
        lane = lanes_of(count)
        return jnp.logical_or(jnp.logical_and(right, lane < 4), jnp.logical_and(left, lane >= 124))

    def blur_sides(at, count, first, last, beyond):
        first, last = halves(first), halves(last)
        beyond = halves(jnp.where(held_lanes(count), beyond, 0.0))
        return (
            col_blur([beyond, first, halves(cov_ref[0, at, :])], g_ref),
            col_blur([halves(cov_ref[1, at, :]), last, beyond], g_ref),
        )

    for v, h, there in corners_in:
        @pl.when(there)
        def _(v=v, h=h):
            corner(v, h).wait_recv()

    lane = lanes_of(5)
    for v, (i, i0) in enumerate(ends):
        first, last, beyond = edges(pl.ds(i0, 16), 16)
        end_ref[0, i : i + 16, :] = end_ref[0, i : i + 16, :] + first
        end_ref[4, i : i + 16, :] = end_ref[4, i : i + 16, :] + last
        end_ref[5, i : i + 16, :] = end_ref[5, i : i + 16, :] + beyond
        low, high = pltpu.roll(corner_in[v, 0], 116, 1), pltpu.roll(corner_in[v, 1], 127, 1)
        rows = slice(4, 9) if v == 0 else slice(23, 28)
        end_ref[0, rows, :] = end_ref[0, rows, :] + jnp.where(lane == 0, low, 0.0)
        end_ref[4, rows, :] = end_ref[4, rows, :] + jnp.where(lane == 127, high, 0.0)
        end_ref[5, rows, :] = end_ref[5, rows, :] + jnp.where(lane >= 124, low, jnp.where(lane < 4, high, 0.0))

    for i, i0 in ends:
        inside = in_window(i0)
        at, part = pl.ds(i0, 16), slice(i, i + 16)
        for k, tile in ((0, 1), (1, 3)):
            cov_ref[k, at, :] = jnp.where(inside, coverage(end_ref[tile, part, :]), 0.0)
        first, last, beyond = (jnp.where(inside, coverage(end_ref[tile, part, :]), 0.0) for tile in (0, 4, 5))
        cb_ref[0, at, :], cb_ref[4, at, :] = blur_sides(at, 16, first, last, beyond)

    @pl.loop(0, 8)
    def _(step):
        u = unit_at(step)
        at = pl.ds(first_row(u), UNIT)
        first, last, beyond = edges(at, UNIT)
        first = coverage(sum_ref[0, at, :] + first)
        last = coverage(sum_ref[1, at, :] + last)
        beyond = coverage(beyond + beyond_own(own_ref[at, :]))
        cb_ref[0, at, :], cb_ref[4, at, :] = blur_sides(at, UNIT, first, last, beyond)

        send_a(u, True)

    own = pltpu.make_async_copy(send_ref.at[col], got_ref.at[col], own_sem)
    own.start()
    dose.wait()

    def finish(c):
        for place, tile in enumerate((1, 2, 3, 0, 4)):
            lanes = pl.ds(pl.multiple_of(TILE * c + 128 * tile, 128), 128)
            out_ref[:, lanes] = dose_ref[:, lanes] * got_ref[c, STRIPE * place : STRIPE * place + STRIPE, :]

    own.wait()

    def received(group, count):
        got = got_ref.at[pl.ds(0, count)]
        pltpu.make_async_copy(got, got, recv_sem.at[group]).wait()

    received(z, 7)
    for s in range(8):
        finish(8 * z + s)

    @pl.loop(1, 4)
    def _(dz):
        group = lax.rem(z + dz, 4)
        received(group, 8)
        for s in range(8):
            finish(8 * group + s)

    @pl.when(down)
    def _():
        row_halo(0).wait_send()

    @pl.when(up)
    def _():
        row_halo(1).wait_send()

    for v, h, there in corners:
        @pl.when(there)
        def _(v=v, h=h):
            corner(v, h).wait_send()

    @pl.when(right)
    def _():
        col_halo(0).wait_send()

    @pl.when(left)
    def _():
        col_halo(1).wait_send()

    for part, rows in enumerate((PART_A, SLOT - PART_A)):
        sent = send_ref.at[pl.ds(0, n_col - 1), pl.ds(0, rows)]
        pltpu.make_async_copy(sent, sent, send_sem.at[part]).wait()


def solution(mesh):
    n_row, n_col = mesh.shape["row"], mesh.shape["col"]
    any_space = pl.BlockSpec(memory_space=pl.ANY)

    def local(level_set, dose_map):
        return pl.pallas_call(
            functools.partial(tile_kernel, n_row, n_col),
            out_shape=jax.ShapeDtypeStruct(dose_map.shape, F32),
            in_specs=[any_space, any_space],
            out_specs=pl.BlockSpec(memory_space=pltpu.VMEM),
            scratch_shapes=[
                pltpu.VMEM((8, PART, FINE), F32),
                pltpu.VMEM((2, 24, FINE), F32),
                pltpu.VMEM((TILES, PART, 128), F32),
                pltpu.VMEM((2, TILES, 48, 128), F32),
                pltpu.VMEM((2, FINE + 48, 128), F32),
                pltpu.VMEM((5, 512, 128), BF16),
                pltpu.VMEM((256, 128), BF16),
                pltpu.VMEM((2, 384, 128), BF16),
                pltpu.VMEM((TILES, UNIT, 128), F32),
                pltpu.VMEM((2, CROWS, 128), F32),
                pltpu.VMEM((2, CROWS, 128), F32),
                pltpu.VMEM((5, CROWS, 128), F32),
                pltpu.VMEM((2, CROWS, 128), F32),
                pltpu.VMEM((HROWS, 128), F32),
                pltpu.VMEM((HROWS, 128), F32),
                pltpu.VMEM((2, HROWS // 128, 5, 128), F32),
                pltpu.VMEM((2, HROWS // 128, 5, 128), F32),
                pltpu.VMEM((6, 32, 128), F32),
                pltpu.VMEM((2, 6, 5, 128), F32),
                pltpu.VMEM((2, 6, 5, 128), F32),
                pltpu.VMEM((2, 5, 128), F32),
                pltpu.VMEM((2, 2, 5, 128), F32),
                pltpu.VMEM((n_col, SLOT, 128), F32),
                pltpu.VMEM((n_col, SLOT, 128), F32),
                pltpu.VMEM(dose_map.shape, F32),
                pltpu.SemaphoreType.DMA((8,)),
                pltpu.SemaphoreType.DMA((2,)),
                pltpu.SemaphoreType.DMA,
                pltpu.SemaphoreType.DMA((2,)),
                pltpu.SemaphoreType.DMA((2,)),
                pltpu.SemaphoreType.DMA((2, 2)),
                pltpu.SemaphoreType.DMA((2, 2)),
                pltpu.SemaphoreType.DMA((2,)),
                pltpu.SemaphoreType.DMA((2,)),
                pltpu.SemaphoreType.DMA((2,)),
                pltpu.SemaphoreType.DMA((4,)),
                pltpu.SemaphoreType.DMA,
            ],
            compiler_params=pltpu.CompilerParams(
                collective_id=0, has_side_effects=True, vmem_limit_bytes=52 << 20
            ),
            name="resample_exchange",
        )(level_set, dose_map)

    return jax.shard_map(
        local,
        mesh=mesh,
        in_specs=(P("row", "col"), P(("row", "col"), None)),
        out_specs=P(("row", "col"), None),
        check_vma=False,
    )
```

```python
import functools
import math

import jax
import jax.numpy as jnp
from jax import lax
from jax.experimental import pallas as pl
from jax.experimental.pallas import tpu as pltpu
from jax.sharding import PartitionSpec as P

F32, BF16 = jnp.float32, jnp.bfloat16
MESH = pl.DeviceIdType.MESH
RAW_TAPS = [math.exp(-0.5 * k * k) for k in range(5)]
TAPS = [t / (RAW_TAPS[0] + 2.0 * sum(RAW_TAPS[1:])) for t in RAW_TAPS]

FINE, TILE, STRIPE = 1600, 640, 20
TILES = 13
PART = 264
UNIT = 96
CROWS = 656
HROWS = 768
BASES = (0, 256, 512, 896, 1152)
SLOT = 100
PART_A = 60


def to_tiles(src_ref, src_at, dst_ref, dst_at, count):
    for tile in range(TILES - 1):
        dst_ref[tile, pl.ds(dst_at, count), :] = src_ref[pl.ds(src_at, count), 128 * tile : 128 * tile + 128]
    dst_ref[12, pl.ds(dst_at, count), 0:64] = src_ref[pl.ds(src_at, count), 1536:1600]


def row_group(x_ref, tile, start, out_ref, out_row):
    a = [x_ref[tile, pl.ds(start + s, 8, stride=5), :] for s in range(-1, 6)]
    even = 3.0 * a[0] + 7.0 * a[1] + 9.0 * a[2] + 5.0 * a[3] + a[4]
    odd = a[2] + 5.0 * a[3] + 9.0 * a[4] + 7.0 * a[5] + 3.0 * a[6]
    out_ref[tile, pl.ds(out_row, 8, stride=2), :] = even
    out_ref[tile, pl.ds(out_row + 1, 8, stride=2), :] = odd


def dot(a, b):
    return jnp.dot(a, b, preferred_element_type=F32)


def tent_dot(rows, w):
    hi = rows.astype(BF16)
    rest = rows - hi.astype(F32)
    mid = rest.astype(BF16)
    low = (rest - mid.astype(F32)).astype(BF16)
    return dot(hi, w) + dot(mid, w) + dot(low, w)


def col_tile(rr_ref, count, w_ref, tile):
    first = BASES[tile] // 128
    return tent_dot(jnp.concatenate([rr_ref[first + t, 0:count, :] for t in range(4)], axis=1), w_ref[tile])


def coverage(total):
    return 1.0 / (1.0 + jnp.exp(total * (-1.0 / 1250.0)))


def halves(cover):
    hi = cover.astype(BF16)
    return hi, (cover - hi.astype(F32)).astype(BF16)


def col_blur(pieces, g_ref):
    hi = jnp.concatenate([p[0] for p in pieces], axis=1)
    low = jnp.concatenate([p[1] for p in pieces], axis=1)
    return dot(hi, g_ref[0]) + dot(low, g_ref[0]) + dot(hi, g_ref[1])


def row_blur(cb_ref, d, tile):
    first = STRIPE * d + 4
    taps = [cb_ref[tile, pl.ds(first + k, STRIPE), :] for k in range(9)]
    total = TAPS[0] * taps[4]
    for k in range(1, 5):
        total = total + TAPS[k] * (taps[4 - k] + taps[4 + k])
    return total


def piece_a(cb_ref, send_ref, d):
    for t in range(3):
        send_ref[d, STRIPE * t : STRIPE * t + STRIPE, :] = row_blur(cb_ref, d, t + 1)


def piece_b(cb_ref, send_ref, d):
    for t in range(2):
        send_ref[d, PART_A + STRIPE * t : PART_A + STRIPE * t + STRIPE, :] = row_blur(cb_ref, d, 4 * t)


def make_weights(w_ref, we_ref, g_ref):
    def tent(fine_col, coarse_col):
        return jnp.maximum(10 - jnp.abs(4 * fine_col - 10 * coarse_col - 3), 0)

    k = lax.broadcasted_iota(jnp.int32, (512, 128), 0)
    n = lax.broadcasted_iota(jnp.int32, (512, 128), 1)
    for tile in range(5):
        w_ref[tile] = tent(k + BASES[tile], n + 128 * tile).astype(F32).astype(BF16)

    k = lax.broadcasted_iota(jnp.int32, (256, 128), 0)
    n = lax.broadcasted_iota(jnp.int32, (256, 128), 1)
    to_left = tent(jnp.where(k < 128, k, k + 1408), n - 1)
    to_right = tent(jnp.where(k < 128, k, k + 1408), n + 628)
    use = jnp.logical_and(n >= 8, n < 13)
    we_ref[...] = jnp.where(n < 5, to_left, jnp.where(use, to_right, 0)).astype(F32).astype(BF16)

    k = lax.broadcasted_iota(jnp.int32, (384, 128), 0)
    n = lax.broadcasted_iota(jnp.int32, (384, 128), 1)
    off = jnp.abs(k - n - 128)
    g = jnp.zeros((384, 128), F32)
    for step in range(5):
        g = jnp.where(off == step, TAPS[step], g)
    hi, low = halves(g)
    g_ref[0] = hi
    g_ref[1] = low


def row_groups(x_ref, start, out_ref, out_row):
    for tile in range(TILES):
        row_group(x_ref, tile, start, out_ref, out_row)


def tile_kernel(
    n_row, n_col, x_hbm, dose_hbm, out_ref,
    x_in, x_ends, x_ref, end_x_ref, side_x_ref, w_ref, we_ref, g_ref, rr_ref, sum_ref, cov_ref, cb_ref,
    strip_ref, own_ref, side_ref, side_out, side_in, end_ref, end_out, end_in,
    corner_out, corner_in, send_ref, got_ref, dose_ref,
    load_sem, end_sem, dose_sem, row_send, row_recv, corner_send, corner_recv, col_send, col_recv, send_sem, recv_sem, own_sem,
):
    row, col = lax.axis_index("row"), lax.axis_index("col")
    z, y, core = col // 8, lax.rem(col // 2, 4), lax.rem(col, 2)
    up, down, left, right = row > 0, row < n_row - 1, col > 0, col < n_col - 1

    def pick(step, values):
        out = values[0]
        for k, value in enumerate(values[1:], 1):
            out = jnp.where(step == k, value, out)
        return out

    def unit_at(step):
        c = lax.rem(z + pick(step, (2, 2, 1, 3, 1, 3, 0, 0)), 4)
        return 2 * c + lax.rem(y // 2 + pick(step, (0, 1, 0, 0, 1, 1, 0, 1)), 2)

    def load_start(u):
        return pl.multiple_of(jnp.clip(200 * u - 24, 0, FINE - PART), 8)

    def load(u):
        return pltpu.make_async_copy(x_hbm.at[pl.ds(load_start(u), PART)], x_in.at[u], load_sem.at[u])

    end_loads = [
        pltpu.make_async_copy(x_hbm.at[pl.ds(at, 24)], x_ends.at[i], end_sem.at[i]) for i, at in enumerate((0, FINE - 24))
    ]
    for end_load in end_loads:
        end_load.start()
    load(unit_at(0)).start()

    side_in[...] = jnp.zeros(side_in.shape, F32)
    end_in[...] = jnp.zeros(end_in.shape, F32)
    corner_in[...] = jnp.zeros(corner_in.shape, F32)

    barrier = pltpu.get_barrier_semaphore()

    @pl.loop(1, n_col, unroll=True)
    def _(k):
        pl.semaphore_signal(barrier, 1, device_id=(row, lax.rem(col + k, n_col)), device_id_type=MESH)

    around = [
        (jnp.logical_and(dv, dh) if dh is not None else dv, row + v, col + h)
        for dv, v in ((up, -1), (down, 1))
        for dh, h in ((None, 0), (left, -1), (right, 1))
    ]
    for there, other_row, other_col in around:
        @pl.when(there)
        def _(other_row=other_row, other_col=other_col):
            pl.semaphore_signal(barrier, 1, device_id=(other_row, other_col), device_id_type=MESH)

    for step in range(1, 8):
        load(unit_at(step)).start()
    dose = pltpu.make_async_copy(dose_hbm, dose_ref, dose_sem)
    dose.start()
    make_weights(w_ref, we_ref, g_ref)
    x_ref[12, :, 64:128] = jnp.zeros((PART, 64), F32)
    end_x_ref[0, :, 0:24, :] = jnp.zeros((TILES, 24, 128), F32)
    end_x_ref[1, :, 24:48, :] = jnp.zeros((TILES, 24, 128), F32)
    end_x_ref[:, 12, :, 64:128] = jnp.zeros((2, 48, 64), F32)
    side_x_ref[:, 0:24, :] = jnp.zeros((2, 24, 128), F32)
    side_x_ref[:, FINE + 24 : FINE + 48, :] = jnp.zeros((2, 24, 128), F32)
    side_x_ref[1, 24 : FINE + 24, 64:128] = jnp.zeros((FINE, 64), F32)
    own_ref[CROWS:HROWS, :] = jnp.zeros((HROWS - CROWS, 128), F32)

    def row_halo(i):
        return pltpu.make_async_remote_copy(
            end_out.at[i], end_in.at[i],
            row_send.at[i], row_recv.at[i], device_id=(row + 1 - 2 * i, col), device_id_type=MESH)

    corners = [(v, h, jnp.logical_and(dv, dh)) for v, dv in ((0, down), (1, up)) for h, dh in ((0, right), (1, left))]
    corners_in = [(v, h, jnp.logical_and(dv, dh)) for v, dv in ((0, up), (1, down)) for h, dh in ((0, left), (1, right))]

    def corner(v, h):
        return pltpu.make_async_remote_copy(
            corner_out.at[v], corner_in.at[v, h],
            corner_send.at[v, h], corner_recv.at[v, h],
            device_id=(row + 1 - 2 * v, col + 1 - 2 * h), device_id_type=MESH)

    def col_halo(i):
        return pltpu.make_async_remote_copy(
            side_out.at[i], side_in.at[i],
            col_send.at[i], col_recv.at[i], device_id=(row, col + 1 - 2 * i), device_id_type=MESH)

    def piece(part, d, slot):
        rows = pl.ds(0, PART_A) if part == 0 else pl.ds(PART_A, SLOT - PART_A)
        return pltpu.make_async_remote_copy(
            send_ref.at[d, rows], got_ref.at[slot, rows],
            send_sem.at[part], recv_sem.at[slot // 8], device_id=(row, d), device_id_type=MESH)

    def stripe(u, s):
        return 4 * u + lax.rem(y + s // 2, 2) * 2 + lax.rem(core + lax.rem(s, 2), 2)

    def first_row(u):
        return pl.multiple_of(16 * jnp.clip(5 * u, 1, 34), 16)

    def resample(u):
        base = load_start(u)

        @pl.loop(0, PART // 24)
        def _(g):
            at = pl.multiple_of(24 * g, 8)
            to_tiles(x_in.at[u], at, x_ref, at, 24)

        first = first_row(u)

        @pl.loop(0, UNIT // 16)
        def _(g):
            row_groups(x_ref, 40 * (first // 16 + g) - 20 - base, rr_ref, 16 * g)

        at = pl.ds(first, UNIT)
        cover = []
        for tile in range(5):
            total = col_tile(rr_ref, UNIT, w_ref, tile)
            if tile in (0, 4):
                sum_ref[tile // 4, at, :] = total
            total = coverage(total)
            if tile in (1, 3):
                cov_ref[tile // 2, at, :] = total
            cover.append(halves(total))
        for tile in range(1, 4):
            cb_ref[tile, at, :] = col_blur(cover[tile - 1 : tile + 2], g_ref)

    def send_a(u, end):
        @pl.loop(0, 4)
        def _(s):
            d = stripe(u, s)
            is_end = jnp.logical_or(d == 0, d == n_col - 1)

            @pl.when(is_end == end)
            def _():
                piece_a(cb_ref, send_ref, d)

                @pl.when(d != col)
                def _():
                    piece(0, d, col).start()

            if end:
                piece_b(cb_ref, send_ref, d)

                @pl.when(d != col)
                def _():
                    piece(1, d, col).start()

    def lanes_of(count):
        return lax.broadcasted_iota(jnp.int32, (count, 128), 1)

    def beyond_own(own):
        lane = lanes_of(own.shape[0])
        return jnp.where(lane == 127, pltpu.roll(own, 127, 1), jnp.where(lane == 0, pltpu.roll(own, 116, 1), 0.0))

    def ends_own():
        for i in range(2):
            end_loads[i].wait()
            to_tiles(x_ends.at[i], 0, end_x_ref.at[i], 24 - 24 * i, 24)
            row_groups(end_x_ref.at[i], 4, rr_ref, 16 * i)
        for tile in range(5):
            end_ref[tile] = col_tile(rr_ref, 32, w_ref, tile)
        own = tent_dot(jnp.concatenate([rr_ref[0, 0:32, :], rr_ref[12, 0:32, :]], axis=1), we_ref[...])
        end_ref[5] = beyond_own(own)
        end_out[0] = end_ref[:, 20:25, :]
        end_out[1] = end_ref[:, 7:12, :]
        corner_out[0] = own[20:25]
        corner_out[1] = own[7:12]

    def send_ends():
        @pl.when(down)
        def _():
            row_halo(0).start()

        @pl.when(up)
        def _():
            row_halo(1).start()

        for v, h, there in corners:
            @pl.when(there)
            def _(v=v, h=h):
                corner(v, h).start()

    def sides():
        for step in range(1, 8):
            load(unit_at(step)).wait()

        @pl.loop(0, 8)
        def _(u):
            for g in range(5):
                source = pl.ds(pl.multiple_of(200 * u - load_start(u) + 40 * g, 8), 40)
                target = pl.ds(pl.multiple_of(24 + 200 * u + 40 * g, 8), 40)
                side_x_ref[0, target, :] = x_in[u, source, 0:128]
                side_x_ref[1, target, 0:64] = x_in[u, source, 1536:1600]

        @pl.loop(0, CROWS // 16)
        def _(g):
            for side in range(2):
                row_group(side_x_ref, side, 4 + 40 * g, strip_ref, 16 * g)

        own_ref[0:CROWS, :] = tent_dot(jnp.concatenate([strip_ref[0], strip_ref[1]], axis=1), we_ref[...])
        for part in range(HROWS // 128):
            columns = jnp.transpose(own_ref[128 * part : 128 * part + 128, :])
            side_out[0, part] = columns[8:13, :]
            side_out[1, part] = columns[0:5, :]

        @pl.when(right)
        def _():
            col_halo(0).start()

        @pl.when(left)
        def _():
            col_halo(1).start()

    ends = ((0, 0), (16, CROWS - 16))

    def in_window(i0):
        j = lax.broadcasted_iota(jnp.int32, (16, 128), 0) + (TILE * row + i0 - 8)
        return jnp.logical_and(j >= 0, j < TILE * n_row)

    def ends_a():
        @pl.when(up)
        def _():
            row_halo(0).wait_recv()

        @pl.when(down)
        def _():
            row_halo(1).wait_recv()

        inside = jnp.concatenate([in_window(i0) for _, i0 in ends], axis=0)
        cover = []
        for tile in range(6):
            end_ref[tile, 4:9, :] = end_ref[tile, 4:9, :] + end_in[0, tile]
            end_ref[tile, 23:28, :] = end_ref[tile, 23:28, :] + end_in[1, tile]
            if tile < 5:
                cover.append(halves(jnp.where(inside, coverage(end_ref[tile]), 0.0)))
        for tile in range(1, 4):
            total = col_blur(cover[tile - 1 : tile + 2], g_ref)
            for i, i0 in ends:
                cb_ref[tile, i0 : i0 + 16, :] = total[i : i + 16]

    ends_own()

    @pl.loop(0, 8)
    def _(step):
        u = unit_at(step)

        @pl.when(step == 0)
        def _():
            load(u).wait()

        resample(u)

        @pl.when(step == 0)
        def _():
            near = n_col - 1
            for there, _, _ in around:
                near = near + there.astype(jnp.int32)
            pl.semaphore_wait(barrier, near)
            send_ends()

        send_a(u, False)

        @pl.when(step == 0)
        def _():
            sides()

    ends_a()

    @pl.when(left)
    def _():
        col_halo(0).wait_recv()

    @pl.when(right)
    def _():
        col_halo(1).wait_recv()

    for part in range(HROWS // 128):
        held = jnp.concatenate(
            [side_in[0, part], jnp.zeros((3, 128), F32), side_in[1, part], jnp.zeros((115, 128), F32)], axis=0)
        side_ref[128 * part : 128 * part + 128, :] = jnp.transpose(held)

    def edges(at, count):
        lane, got = lanes_of(count), side_ref[at, :]
        low, high = pltpu.roll(got, 124, 1), pltpu.roll(got, 119, 1)
        beyond = jnp.where(lane >= 124, low, jnp.where(lane < 4, high, 0.0))
        return jnp.where(lane == 0, low, 0.0), jnp.where(lane == 127, high, 0.0), beyond

    def held_lanes(count):
        lane = lanes_of(count)
        return jnp.logical_or(jnp.logical_and(right, lane < 4), jnp.logical_and(left, lane >= 124))

    def blur_sides(at, count, first, last, beyond):
        first, last = halves(first), halves(last)
        beyond = halves(jnp.where(held_lanes(count), beyond, 0.0))
        return (
            col_blur([beyond, first, halves(cov_ref[0, at, :])], g_ref),
            col_blur([halves(cov_ref[1, at, :]), last, beyond], g_ref),
        )

    for v, h, there in corners_in:
        @pl.when(there)
        def _(v=v, h=h):
            corner(v, h).wait_recv()

    lane = lanes_of(5)
    for v, (i, i0) in enumerate(ends):
        first, last, beyond = edges(pl.ds(i0, 16), 16)
        end_ref[0, i : i + 16, :] = end_ref[0, i : i + 16, :] + first
        end_ref[4, i : i + 16, :] = end_ref[4, i : i + 16, :] + last
        end_ref[5, i : i + 16, :] = end_ref[5, i : i + 16, :] + beyond
        low, high = pltpu.roll(corner_in[v, 0], 116, 1), pltpu.roll(corner_in[v, 1], 127, 1)
        rows = slice(4, 9) if v == 0 else slice(23, 28)
        end_ref[0, rows, :] = end_ref[0, rows, :] + jnp.where(lane == 0, low, 0.0)
        end_ref[4, rows, :] = end_ref[4, rows, :] + jnp.where(lane == 127, high, 0.0)
        end_ref[5, rows, :] = end_ref[5, rows, :] + jnp.where(lane >= 124, low, jnp.where(lane < 4, high, 0.0))

    for i, i0 in ends:
        inside = in_window(i0)
        at, part = pl.ds(i0, 16), slice(i, i + 16)
        for k, tile in ((0, 1), (1, 3)):
            cov_ref[k, at, :] = jnp.where(inside, coverage(end_ref[tile, part, :]), 0.0)
        first, last, beyond = (jnp.where(inside, coverage(end_ref[tile, part, :]), 0.0) for tile in (0, 4, 5))
        cb_ref[0, at, :], cb_ref[4, at, :] = blur_sides(at, 16, first, last, beyond)

    @pl.loop(0, 8)
    def _(step):
        u = unit_at(step)
        at = pl.ds(first_row(u), UNIT)
        first, last, beyond = edges(at, UNIT)
        first = coverage(sum_ref[0, at, :] + first)
        last = coverage(sum_ref[1, at, :] + last)
        beyond = coverage(beyond + beyond_own(own_ref[at, :]))
        cb_ref[0, at, :], cb_ref[4, at, :] = blur_sides(at, UNIT, first, last, beyond)

        send_a(u, True)

    own = pltpu.make_async_copy(send_ref.at[col], got_ref.at[col], own_sem)
    own.start()
    dose.wait()

    def finish(c):
        for place, tile in enumerate((1, 2, 3, 0, 4)):
            lanes = pl.ds(pl.multiple_of(TILE * c + 128 * tile, 128), 128)
            out_ref[:, lanes] = dose_ref[:, lanes] * got_ref[c, STRIPE * place : STRIPE * place + STRIPE, :]

    own.wait()

    def received(group, count):
        got = got_ref.at[pl.ds(0, count)]
        pltpu.make_async_copy(got, got, recv_sem.at[group]).wait()

    received(z, 7)
    for s in range(8):
        finish(8 * z + s)

    @pl.loop(1, 4)
    def _(dz):
        group = lax.rem(z + dz, 4)
        received(group, 8)
        for s in range(8):
            finish(8 * group + s)

    @pl.when(down)
    def _():
        row_halo(0).wait_send()

    @pl.when(up)
    def _():
        row_halo(1).wait_send()

    for v, h, there in corners:
        @pl.when(there)
        def _(v=v, h=h):
            corner(v, h).wait_send()

    @pl.when(right)
    def _():
        col_halo(0).wait_send()

    @pl.when(left)
    def _():
        col_halo(1).wait_send()

    for part, rows in enumerate((PART_A, SLOT - PART_A)):
        sent = send_ref.at[pl.ds(0, n_col - 1), pl.ds(0, rows)]
        pltpu.make_async_copy(sent, sent, send_sem.at[part]).wait()


def solution(mesh):
    n_row, n_col = mesh.shape["row"], mesh.shape["col"]
    any_space = pl.BlockSpec(memory_space=pl.ANY)

    def local(level_set, dose_map):
        return pl.pallas_call(
            functools.partial(tile_kernel, n_row, n_col),
            out_shape=jax.ShapeDtypeStruct(dose_map.shape, F32),
            in_specs=[any_space, any_space],
            out_specs=pl.BlockSpec(memory_space=pltpu.VMEM),
            scratch_shapes=[
                pltpu.VMEM((8, PART, FINE), F32),
                pltpu.VMEM((2, 24, FINE), F32),
                pltpu.VMEM((TILES, PART, 128), F32),
                pltpu.VMEM((2, TILES, 48, 128), F32),
                pltpu.VMEM((2, FINE + 48, 128), F32),
                pltpu.VMEM((5, 512, 128), BF16),
                pltpu.VMEM((256, 128), BF16),
                pltpu.VMEM((2, 384, 128), BF16),
                pltpu.VMEM((TILES, UNIT, 128), F32),
                pltpu.VMEM((2, CROWS, 128), F32),
                pltpu.VMEM((2, CROWS, 128), F32),
                pltpu.VMEM((5, CROWS, 128), F32),
                pltpu.VMEM((2, CROWS, 128), F32),
                pltpu.VMEM((HROWS, 128), F32),
                pltpu.VMEM((HROWS, 128), F32),
                pltpu.VMEM((2, HROWS // 128, 5, 128), F32),
                pltpu.VMEM((2, HROWS // 128, 5, 128), F32),
                pltpu.VMEM((6, 32, 128), F32),
                pltpu.VMEM((2, 6, 5, 128), F32),
                pltpu.VMEM((2, 6, 5, 128), F32),
                pltpu.VMEM((2, 5, 128), F32),
                pltpu.VMEM((2, 2, 5, 128), F32),
                pltpu.VMEM((n_col, SLOT, 128), F32),
                pltpu.VMEM((n_col, SLOT, 128), F32),
                pltpu.VMEM(dose_map.shape, F32),
                pltpu.SemaphoreType.DMA((8,)),
                pltpu.SemaphoreType.DMA((2,)),
                pltpu.SemaphoreType.DMA,
                pltpu.SemaphoreType.DMA((2,)),
                pltpu.SemaphoreType.DMA((2,)),
                pltpu.SemaphoreType.DMA((2, 2)),
                pltpu.SemaphoreType.DMA((2, 2)),
                pltpu.SemaphoreType.DMA((2,)),
                pltpu.SemaphoreType.DMA((2,)),
                pltpu.SemaphoreType.DMA((2,)),
                pltpu.SemaphoreType.DMA((4,)),
                pltpu.SemaphoreType.DMA,
            ],
            compiler_params=pltpu.CompilerParams(
                collective_id=0, has_side_effects=True, vmem_limit_bytes=52 << 20
            ),
            name="resample_exchange",
        )(level_set, dose_map)

    return jax.shard_map(
        local,
        mesh=mesh,
        in_specs=(P("row", "col"), P(("row", "col"), None)),
        out_specs=P(("row", "col"), None),
        check_vma=False,
    )
```
